32 devices in a mesh: dp: 16 (over z, y, x), seq: 2 (over core).
Axes of the slice: x: 2, y: 2, z: 4, core: 2. Of those that a mesh axis runs over, the one named last changes fastest.
Arguments:
- latents: bfloat16 [16, 1024, 1152], P('dp', 'seq'), may hold values from -6 to 6
- condition: bfloat16 [16, 1152], P('dp'), may hold values from -6 to 6
- cotangent: bfloat16 [16, 1024, 1152], P('dp', 'seq'), may hold values from -6 to 6
- teacher: bfloat16 [16, 1024, 1152], P('dp', 'seq'), may hold values from -6 to 6
- valid_mask: int32 [16, 1024], P('dp', 'seq'), may hold values from 0 to 1, as said below
- modulation_weight: float32 [1152, 6912], P('seq', 'dp'), may hold values from -0.1875 to 0.1875
- attention_weight: float32 [1152, 3456], P('seq', 'dp'), may hold values from -0.1875 to 0.1875
- projection_weight: float32 [1152, 1152], P('seq', 'dp'), may hold values from -0.5 to 0.5
- expansion_weight: float32 [1152, 4608], P('seq', 'dp'), may hold values from -0.1875 to 0.1875
- contraction_weight: float32 [4608, 1152], P('seq', 'dp'), may hold values from -0.125 to 0.125
- modulation_moment: float32 [1152, 6912], P('seq', 'dp'), may hold values from -224 to 224
- attention_moment: float32 [1152, 3456], P('seq', 'dp'), may hold values from -80 to 80
- projection_moment: float32 [1152, 1152], P('seq', 'dp'), may hold values from -160 to 160
- expansion_moment: float32 [1152, 4608], P('seq', 'dp'), may hold values from -224 to 224
- contraction_moment: float32 [4608, 1152], P('seq', 'dp'), may hold values from -320 to 320
- modulation_average: float32 [1152, 6912], P('seq', 'dp'), may hold values from -0.1875 to 0.1875
- attention_average: float32 [1152, 3456], P('seq', 'dp'), may hold values from -0.1875 to 0.1875
- projection_average: float32 [1152, 1152], P('seq', 'dp'), may hold values from -0.5 to 0.5
- expansion_average: float32 [1152, 4608], P('seq', 'dp'), may hold values from -0.1875 to 0.1875
- contraction_average: float32 [4608, 1152], P('seq', 'dp'), may hold values from -0.125 to 0.125
Outputs:
- block_output: float32 [16, 1024, 1152], P('dp', 'seq')
- masked_loss: float32 [], replicated
- latent_grad: float32 [16, 1024, 1152], P('dp', 'seq')
- condition_grad: float32 [16, 1152], P('dp')
- modulation_next: float32 [1152, 6912], P('seq', 'dp')
- attention_next: float32 [1152, 3456], P('seq', 'dp')
- projection_next: float32 [1152, 1152], P('seq', 'dp')
- expansion_next: float32 [1152, 4608], P('seq', 'dp')
- contraction_next: float32 [4608, 1152], P('seq', 'dp')
- modulation_moment_next: float32 [1152, 6912], P('seq', 'dp')
- attention_moment_next: float32 [1152, 3456], P('seq', 'dp')
- projection_moment_next: float32 [1152, 1152], P('seq', 'dp')
- expansion_moment_next: float32 [1152, 4608], P('seq', 'dp')
- contraction_moment_next: float32 [4608, 1152], P('seq', 'dp')
- modulation_average_next: float32 [1152, 6912], P('seq', 'dp')
- attention_average_next: float32 [1152, 3456], P('seq', 'dp')
- projection_average_next: float32 [1152, 1152], P('seq', 'dp')
- expansion_average_next: float32 [1152, 4608], P('seq', 'dp')
- contraction_average_next: float32 [4608, 1152], P('seq', 'dp')
The draws below stay inside these ranges and needn't reach their ends.
Inputs may be any that keep to these rules, and one draw needn't show every extreme that they name: `valid_mask`: the first token of every latent is valid.
All inputs are finite; a program needn't handle non-finite values.
Results may differ from the reference program's by a relative error of at most 0.02.
The reference program's roundings to bfloat16 on the way count: a program that leaves them out, or rounds other values in their place, can miss the bound.
Values may be sent and summed in bfloat16 or wider, within the bound.
No kernel may reach another device: no remote copies, remote signals or barrier semaphores. Data moves between devices by JAX's collectives and lax.ppermute only.
A program may use at most 320 MiB of HBM per device.

```python
import math
import jax
import jax.numpy as jnp
from jax import lax

D = 1152
HEADS = 16
FF = 4608
SEQ_LEN = 1024
LATENTS = 16


def draw_valid_mask(key, part):
    key = jax.random.fold_in(key, 7)
    latent_index = jnp.arange(LATENTS, dtype=jnp.int32)[:, None]
    position = jnp.arange(SEQ_LEN, dtype=jnp.int32)[None, :]
    threshold = 100 * (LATENTS + 2 * latent_index) // LATENTS * (SEQ_LEN + 2 * position) // SEQ_LEN
    rolled = jax.random.randint(key, (LATENTS, SEQ_LEN), 0, 1000, dtype=jnp.int32)
    marked = jnp.where(rolled < threshold, 1, 0).astype(jnp.int32)
    return jnp.where(position == 0, 1, marked).astype(jnp.int32)


def block_levels(rng, shape, cuts, smallest, largest):
    level, own = 1.0, jax.random.fold_in(rng, 6)
    for dim, parts in cuts:
        heights = jnp.exp(jax.random.uniform(jax.random.fold_in(own, dim), (parts,), jnp.float32, smallest / len(cuts), largest / len(cuts)))
        level = level * jnp.repeat(heights, shape[dim] // parts).reshape([-1 if axis == dim else 1 for axis in range(len(shape))])
    return level


def bell_draw(own_key, dims, spread, most, pieces=(), kind=jnp.bfloat16):
    array = jax.random.normal(own_key, dims, jnp.float32) * spread
    if len(pieces) > 0:
        array = block_levels(own_key, dims, pieces, -0.22, 0.18) * array
    return jnp.clip(array, min=-most, max=most).astype(kind)


def setup_inputs(seed: int = 0) -> dict:
    streams_of = jax.random.split(jax.random.key(seed), 21)
    return {
        "latents": bell_draw(streams_of[0], (LATENTS, SEQ_LEN, D), 1.0, 6.0, ((0, 16), (1, 2))),
        "condition": bell_draw(streams_of[1], (LATENTS, D), 1.0, 6.0, ((0, 16),)),
        "cotangent": bell_draw(streams_of[2], (LATENTS, SEQ_LEN, D), 1.0, 6.0, ((0, 16), (1, 2))),
        "teacher": bell_draw(streams_of[3], (LATENTS, SEQ_LEN, D), 1.0, 6.0, ((0, 16), (1, 2))),
        "valid_mask": draw_valid_mask(jax.random.fold_in(streams_of[20], 71), 0),
        "modulation_weight": bell_draw(streams_of[5], (D, 6 * D), D ** -0.5, 0.1875, ((0, 2), (1, 16)), jnp.float32),
        "attention_weight": bell_draw(streams_of[6], (D, 3 * D), D ** -0.5, 0.1875, ((0, 2), (1, 16)), jnp.float32),
        "projection_weight": bell_draw(streams_of[7], (D, D), (D // 8) ** -0.5, 0.5, ((0, 2), (1, 16)), jnp.float32),
        "expansion_weight": bell_draw(streams_of[8], (D, FF), D ** -0.5, 0.1875, ((0, 2), (1, 16)), jnp.float32),
        "contraction_weight": bell_draw(streams_of[9], (FF, D), (FF // 2) ** -0.5, 0.125, ((0, 2), (1, 16)), jnp.float32),
        "modulation_moment": bell_draw(streams_of[10], (D, 6 * D), (0.3 * (LATENTS * SEQ_LEN) ** 0.5), 224.0, ((0, 2), (1, 16)), jnp.float32),
        "attention_moment": bell_draw(streams_of[11], (D, 3 * D), (0.1 * (LATENTS * SEQ_LEN) ** 0.5), 80.0, ((0, 2), (1, 16)), jnp.float32),
        "projection_moment": bell_draw(streams_of[12], (D, D), (0.2 * (LATENTS * SEQ_LEN) ** 0.5), 160.0, ((0, 2), (1, 16)), jnp.float32),
        "expansion_moment": bell_draw(streams_of[13], (D, FF), (0.3 * (LATENTS * SEQ_LEN) ** 0.5), 224.0, ((0, 2), (1, 16)), jnp.float32),
        "contraction_moment": bell_draw(streams_of[14], (FF, D), (0.4 * (LATENTS * SEQ_LEN) ** 0.5), 320.0, ((0, 2), (1, 16)), jnp.float32),
        "modulation_average": bell_draw(streams_of[15], (D, 6 * D), D ** -0.5, 0.1875, ((0, 2), (1, 16)), jnp.float32),
        "attention_average": bell_draw(streams_of[16], (D, 3 * D), D ** -0.5, 0.1875, ((0, 2), (1, 16)), jnp.float32),
        "projection_average": bell_draw(streams_of[17], (D, D), (D // 8) ** -0.5, 0.5, ((0, 2), (1, 16)), jnp.float32),
        "expansion_average": bell_draw(streams_of[18], (D, FF), D ** -0.5, 0.1875, ((0, 2), (1, 16)), jnp.float32),
        "contraction_average": bell_draw(streams_of[19], (FF, D), (FF // 2) ** -0.5, 0.125, ((0, 2), (1, 16)), jnp.float32),
    }


epsilon = 1e-06
highest = lax.Precision.HIGHEST

@jax.custom_vjp
def low(v):
    return lax.optimization_barrier(v.astype(jnp.bfloat16)).astype(jnp.float32)

@jax.custom_vjp
def low_back(v):
    return v

def low_keep(v):
    return (low(v), None)

def low_pass(kept, grad):
    return (grad,)

def back_keep(v):
    return (v, None)

def back_low(kept, grad):
    return (low(grad),)
low.defvjp(low_keep, low_pass)
low_back.defvjp(back_keep, back_low)

def silu_of(values):
    return values * jax.nn.sigmoid(values)

def gelu_of(values):
    tanh_input = 0.7978845608028654 * (values + 0.044715 * values * values * values)
    return 0.5 * values * (1.0 + jnp.tanh(tanh_input))

def modulated(values, offset, stretch):
    centered = values - lax.optimization_barrier(jnp.mean(values, axis=-1, keepdims=True))
    variance = lax.optimization_barrier(jnp.mean(centered * centered, axis=-1, keepdims=True))
    return centered * lax.rsqrt(variance + epsilon) * (1.0 + stretch) + offset

def latent_block(residual_in, cond_values, modulation_weight, attention_weight, projection_weight, expansion_weight, contraction_weight):
    model_width = residual_in.shape[-1]
    head_size = model_width // HEADS
    score_scale = head_size ** (-0.5)
    cond_active = low(silu_of(cond_values))
    modulation = low_back(jnp.dot(cond_active[None, :], low(modulation_weight), precision=highest))
    shift_attn, scale_attn, gate_attn, shift_mlp, scale_mlp, gate_mlp = jnp.split(modulation, 6, axis=-1)
    attn_input = low(modulated(residual_in, shift_attn, scale_attn))
    qkv_values = low(low_back(jnp.dot(attn_input, low(attention_weight), precision=highest)))
    query_heads = qkv_values[:, :model_width].reshape(SEQ_LEN, HEADS, head_size)
    key_heads = qkv_values[:, model_width:2 * model_width].reshape(SEQ_LEN, HEADS, head_size)
    value_heads = qkv_values[:, 2 * model_width:].reshape(SEQ_LEN, HEADS, head_size)
    scores = low_back(jnp.einsum('qhd,khd->hqk', query_heads, key_heads, precision=highest) * score_scale)
    top_score = lax.optimization_barrier(jnp.max(scores, axis=-1, keepdims=True))
    raised = jnp.exp(scores - top_score)
    probabilities = raised / lax.optimization_barrier(jnp.sum(raised, axis=-1, keepdims=True))
    attn_out = jnp.einsum('hqk,khd->qhd', low(probabilities), value_heads, precision=highest)
    attn_low = low(low_back(attn_out.reshape(SEQ_LEN, model_width)))
    proj_out = low_back(jnp.dot(attn_low, low(projection_weight), precision=highest))
    mid_resid = residual_in + gate_attn * proj_out
    mlp_input = low(modulated(mid_resid, shift_mlp, scale_mlp))
    hidden_pre = low_back(jnp.dot(mlp_input, low(expansion_weight), precision=highest))
    hidden_low = low(gelu_of(hidden_pre))
    mlp_out = low_back(jnp.dot(hidden_low, low(contraction_weight), precision=highest))
    return mid_resid + gate_mlp * mlp_out

def reference(latents, condition, cotangent, teacher, valid_mask, modulation_weight, attention_weight, projection_weight, expansion_weight, contraction_weight, modulation_moment, attention_moment, projection_moment, expansion_moment, contraction_moment, modulation_average, attention_average, projection_average, expansion_average, contraction_average):
    masters = (modulation_weight, attention_weight, projection_weight, expansion_weight, contraction_weight)
    moments = (modulation_moment, attention_moment, projection_moment, expansion_moment, contraction_moment)
    averages = (modulation_average, attention_average, projection_average, expansion_average, contraction_average)
    count_total = jnp.sum(valid_mask.astype(jnp.float32))
    model_width = latents.shape[-1]

    def one_latent(running, latent_items):
        latent_in, cond_in, cot_in, teacher_in, mask_in = latent_items

        def objective(residual_in, cond_values, weight_set):
            block_out = latent_block(residual_in, cond_values, *weight_set)
            teacher_gap = block_out - teacher_in.astype(jnp.float32)
            square = jnp.sum(mask_in.astype(jnp.float32)[:, None] * teacher_gap * teacher_gap)
            return (block_out, square / (count_total * model_width))
        (block_out, partial_loss), pullback = jax.vjp(objective, latent_in.astype(jnp.float32), cond_in.astype(jnp.float32), masters)
        latent_part, cond_part, weight_parts = pullback((cot_in.astype(jnp.float32), jnp.ones((), jnp.float32)))
        running = tuple((current + increment for current, increment in zip(running, weight_parts)))
        return (running, (block_out, partial_loss, latent_part, cond_part))
    zeros_init = tuple((jnp.zeros_like(master) for master in masters))
    weight_grads, (block_output, partial_losses, latent_grad, condition_grad) = lax.scan(one_latent, zeros_init, (latents, condition, cotangent, teacher, valid_mask))
    masked_loss = jnp.sum(partial_losses)
    step_rate = 0.06 / math.sqrt(LATENTS * SEQ_LEN)
    weight_next = []
    moment_next = []
    average_next = []
    for master, gradient, moment, average in zip(masters, weight_grads, moments, averages):
        moment_new = 0.5 * moment + gradient
        master_new = master - step_rate * (gradient + 0.5 * moment_new)
        weight_next.append(master_new)
        moment_next.append(moment_new)
        average_next.append(0.5 * average + 0.5 * master_new)
    return (block_output, masked_loss, latent_grad, condition_grad, weight_next[0], weight_next[1], weight_next[2], weight_next[3], weight_next[4], moment_next[0], moment_next[1], moment_next[2], moment_next[3], moment_next[4], average_next[0], average_next[1], average_next[2], average_next[3], average_next[4])
```

```python
import math

import jax
import jax.numpy as jnp
from jax import lax
from jax.experimental import pallas as pl
from jax.experimental.pallas import tpu as pltpu
from jax.sharding import PartitionSpec as P

HEADS = 16
SEQ_LEN = 1024

epsilon = 1e-06
low = jnp.bfloat16


def silu_of(values):
    return values * jax.nn.sigmoid(values)


def gelu_of(values):
    tanh_input = 0.7978845608028654 * (values + 0.044715 * values * values * values)
    return 0.5 * values * (1.0 + jnp.tanh(tanh_input))


def modulated(values, offset, stretch):
    centered = values - jnp.mean(values, axis=-1, keepdims=True)
    variance = jnp.mean(centered * centered, axis=-1, keepdims=True)
    return centered * lax.rsqrt(variance + epsilon) * (1.0 + stretch) + offset


def dot(first, second, over):
    return lax.dot_general(first, second, (over, ((), ())), preferred_element_type=jnp.float32)


def nn(first, second):
    return dot(first, second, ((1,), (0,)))


def nt(first, second):
    return dot(first, second, ((1,), (1,)))


def tn(first, second):
    return dot(first, second, ((0,), (0,)))


def around(pieces):
    size = lax.axis_size("seq")
    got = [pieces[0]] * size
    for r in range(1, size):
        steps = [(j, (j + r) % size) for j in range(size)]
        got[(size - r) % size] = lax.ppermute(pieces[r], "seq", steps)
    return got


def in_order(got):
    size = lax.axis_size("seq")
    me = lax.axis_index("seq")
    if size == 2:
        return [jnp.where(me == 0, got[0], got[1]), jnp.where(me == 0, got[1], got[0])]
    stacked = jnp.stack(got)
    return [lax.dynamic_index_in_dim(stacked, (j - me) % size, 0, False) for j in range(size)]


def by_distance(array, axis):
    size = lax.axis_size("seq")
    me = lax.axis_index("seq")
    return [lax.dynamic_index_in_dim(array, (me + r) % size, axis, False) for r in range(size)]


def gather_tokens(own):
    return jnp.concatenate(around([own] * lax.axis_size("seq")), axis=0)


def sum_tokens(parts):
    return sum(around(parts))


def swap(array, bit):
    size = lax.axis_size("dp")
    return lax.ppermute(array, "dp", [(j, j ^ bit) for j in range(size)])


def hypercube():
    size = lax.axis_size("dp")
    return size >= 4 and size & (size - 1) == 0


def place(pieces, distances):
    size = lax.axis_size("dp")
    index = jnp.array(distances, jnp.int32) ^ lax.axis_index("dp").astype(jnp.int32)
    each = size // len(pieces)

    def kernel(index_ref, *refs):
        sources, target, arrived = refs[: len(pieces)], refs[-2], refs[-1]
        copies = []
        for n in range(size):
            copy = pltpu.make_async_copy(
                sources[n // each].at[n % each], target.at[index_ref[n]], arrived.at[n]
            )
            copy.start()
            copies.append(copy)
        for copy in copies:
            copy.wait()

    whole = (size,) + pieces[0].shape[1:]
    return pl.pallas_call(
        kernel,
        out_shape=jax.ShapeDtypeStruct(whole, pieces[0].dtype),
        in_specs=[pl.BlockSpec(memory_space=pltpu.SMEM)]
        + [pl.BlockSpec(memory_space=pl.ANY)] * len(pieces),
        out_specs=pl.BlockSpec(memory_space=pl.ANY),
        scratch_shapes=[pltpu.SemaphoreType.DMA((size,))],
        cost_estimate=pl.CostEstimate(
            flops=0, bytes_accessed=2 * math.prod(whole) * 2, transcendentals=0
        ),
    )(index, *pieces)


def gather_columns(shard, first, last):
    size = lax.axis_size("dp")
    if not hypercube():
        return lax.all_gather(shard, "dp", axis=0)
    held, distances = shard[None], [0]
    bit = size >> 1
    while bit >= 4:
        held = jnp.concatenate([held, swap(held, bit)], axis=0)
        distances = distances + [d ^ bit for d in distances]
        bit >>= 1
    by_first = swap(held, first)
    by_last = swap(held, last)
    by_both = swap(by_first, last)
    order = [d ^ step for step in (0, first, last, first | last) for d in distances]
    return place([held, by_first, by_last, by_both], order)


def sum_columns(blocks, first, last):
    size = lax.axis_size("dp")
    if not hypercube():
        return lax.psum_scatter(blocks, "dp", scatter_dimension=0, tiled=False)
    me = lax.axis_index("dp")
    shape = blocks.shape[1:]
    split = blocks.reshape((size // 4, 2, 2) + shape)

    def group(distance):
        want = (me ^ distance) & 3
        part = lax.dynamic_slice(
            split, (0, want >> 1, want & 1) + (0,) * len(shape), (size // 4, 1, 1) + shape
        )
        return part.reshape((size // 4,) + shape)

    def plus(a, b):
        return (a.astype(jnp.float32) + b.astype(jnp.float32)).astype(a.dtype)

    far = swap(group(first | last), first)
    near = swap(group(first), first)
    through = swap(plus(group(last), far), last)
    held = plus(plus(group(0), near), through)
    bit = 4
    while bit < size:
        pairs = held.reshape((held.shape[0] // 2, 2) + shape)
        mine = (me // bit) & 1
        away = lax.dynamic_index_in_dim(pairs, 1 - mine, 1, False)
        held = plus(lax.dynamic_index_in_dim(pairs, mine, 1, False), swap(away, bit))
        bit <<= 1
    return held[0]


def body(
    latents,
    condition,
    cotangent,
    teacher,
    valid_mask,
    modulation_weight,
    attention_weight,
    projection_weight,
    expansion_weight,
    contraction_weight,
    modulation_moment,
    attention_moment,
    projection_moment,
    expansion_moment,
    contraction_moment,
    modulation_average,
    attention_average,
    projection_average,
    expansion_average,
    contraction_average,
):
    local_latents, block_rows, width = latents.shape
    seq_size, dp_size = lax.axis_size("seq"), lax.axis_size("dp")
    seq_me, dp_me = lax.axis_index("seq"), lax.axis_index("dp")
    all_latents = local_latents * dp_size
    head_size = width // HEADS
    heads = HEADS // seq_size
    own_width = heads * head_size
    score_scale = head_size ** (-0.5)
    own_tokens = local_latents * block_rows
    tokens = own_tokens * seq_size
    row_share = attention_weight.shape[0]
    mod_share = modulation_weight.shape[1]
    qkv_share = attention_weight.shape[1]
    proj_share = projection_weight.shape[1]
    hidden_share = expansion_weight.shape[1]
    hidden_piece = hidden_share // seq_size

    attention_low = attention_weight.astype(low).T
    projection_low = projection_weight.astype(low).T
    small = jnp.concatenate([attention_low, projection_low], axis=0)
    half = small.shape[0] // 2
    small_a = gather_columns(small[:half], 1, 2)
    small_b = gather_columns(small[half:], 2, 1)

    expansion_low = expansion_weight.astype(low).T.reshape(seq_size, hidden_piece, row_share)
    expansion_shard = jnp.concatenate(in_order(around(by_distance(expansion_low, 0))), axis=1)
    contraction_low = contraction_weight.astype(low).reshape(
        dp_size // seq_size, seq_size, hidden_piece, proj_share
    )
    contraction_shard = jnp.concatenate(in_order(around(by_distance(contraction_low, 1))), axis=0)
    contraction_shard = contraction_shard.reshape(dp_size * hidden_piece, proj_share).T
    expansion_full = gather_columns(expansion_shard, 1, 2).reshape(dp_size * hidden_piece, width)
    contraction_full = gather_columns(contraction_shard, 2, 1).reshape(
        width, dp_size * hidden_piece
    )

    small_full = jnp.concatenate([small_a, small_b], axis=1)
    projection_full = small_full[:, qkv_share:].reshape(width, own_width)
    attention_rows = small_full[:, :qkv_share].reshape(3, seq_size, own_width, row_share)
    attention_full = jnp.concatenate(
        in_order(around(by_distance(attention_rows, 1))), axis=-1
    ).reshape(3 * own_width, width)

    mask_float = valid_mask.astype(jnp.float32)
    chunk = math.gcd(own_tokens, 128)
    counts = jnp.sum(mask_float.reshape(own_tokens // chunk, chunk), axis=1).astype(low)
    packed = lax.all_gather(
        jnp.concatenate([condition.reshape(-1), counts])[None], ("dp", "seq"), axis=0, tiled=True
    ).reshape(dp_size, seq_size, -1)
    count_total = jnp.sum(packed[:, :, local_latents * width :].astype(jnp.float32))
    every_cond = packed[:, 0, : local_latents * width].reshape(all_latents, width)
    cond_active = silu_of(every_cond.astype(jnp.float32)).astype(low)
    cond_rows = lax.dynamic_slice(
        cond_active, (0, seq_me * row_share), (all_latents, row_share)
    )
    modulation_low = modulation_weight.astype(low)
    mod_part = nn(cond_rows, modulation_low).reshape(dp_size, local_latents, mod_share)
    mod_part = lax.all_to_all(mod_part, "dp", 0, 0, tiled=True)
    modulation = sum(around([mod_part] * seq_size))
    modulation = jnp.transpose(modulation, (1, 0, 2)).reshape(local_latents, dp_size * mod_share)
    shift_attn, scale_attn, gate_attn, shift_mlp, scale_mlp, gate_mlp = [
        group[:, None, :] for group in jnp.split(modulation, 6, axis=-1)
    ]

    residual_in = latents.astype(jnp.float32)
    attn_value, attn_pull = jax.vjp(modulated, residual_in, shift_attn, scale_attn)
    attn_input = gather_tokens(attn_value.astype(low).reshape(own_tokens, width))
    qkv_low = nt(attn_input, attention_full).astype(low)

    def to_heads(array):
        array = array.reshape(seq_size, local_latents, block_rows, heads, head_size)
        return jnp.transpose(array, (1, 0, 2, 3, 4)).reshape(
            local_latents, seq_size * block_rows, heads, head_size
        )

    def from_heads(array):
        array = array.reshape(local_latents, seq_size, block_rows, own_width)
        return jnp.transpose(array, (1, 0, 2, 3)).reshape(tokens, own_width)

    query, key, value = [
        to_heads(qkv_low[:, n * own_width : (n + 1) * own_width]) for n in range(3)
    ]
    scores = (
        jnp.einsum("lqhd,lkhd->lhqk", query, key, preferred_element_type=jnp.float32) * score_scale
    )
    top = jnp.max(scores, axis=-1)
    raised = jnp.exp(scores - top[..., None])
    total = jnp.sum(raised, axis=-1)
    weighted = jnp.einsum(
        "lhqk,lkhd->lqhd", raised.astype(low), value, preferred_element_type=jnp.float32
    )
    attn_out = weighted / jnp.transpose(total, (0, 2, 1))[..., None]
    log_total = top + jnp.log(total)
    attn_low = from_heads(attn_out.astype(low))

    def by_block(array):
        return [array[r * own_tokens : (r + 1) * own_tokens] for r in range(seq_size)]

    def own_shape(array):
        return array.reshape(local_latents, block_rows, width)

    proj_out = own_shape(sum_tokens([nt(rows, projection_full) for rows in by_block(attn_low)]))
    mid_resid = residual_in + gate_attn * proj_out

    mlp_value, mlp_pull = jax.vjp(modulated, mid_resid, shift_mlp, scale_mlp)
    mlp_input = gather_tokens(mlp_value.astype(low).reshape(own_tokens, width))
    hidden_pre = nt(mlp_input, expansion_full)
    gelu_value, gelu_pull = jax.vjp(gelu_of, hidden_pre)
    hidden_low = gelu_value.astype(low)
    mlp_out = own_shape(sum_tokens([nt(rows, contraction_full) for rows in by_block(hidden_low)]))
    block_output = mid_resid + gate_mlp * mlp_out

    teacher_gap = block_output - teacher.astype(jnp.float32)
    local_square = jnp.sum(mask_float[..., None] * teacher_gap * teacher_gap)
    out_grad = cotangent.astype(jnp.float32) + 2.0 * mask_float[..., None] * teacher_gap / (
        count_total * width
    )

    gate_mlp_grad = jnp.sum(out_grad * mlp_out, axis=1)
    mlp_out_grad = gather_tokens((gate_mlp * out_grad).astype(low).reshape(own_tokens, width))
    contraction_grad = tn(mlp_out_grad, hidden_low).astype(low)
    contraction_sum = sum_columns(
        contraction_grad.reshape(dp_size, proj_share, dp_size * hidden_piece), 1, 2
    )
    hidden_grad = nn(mlp_out_grad, contraction_full)
    hidden_pre_grad = gelu_pull(hidden_grad)[0].astype(low)
    expansion_grad = tn(hidden_pre_grad, mlp_input).astype(low)
    expansion_sum = sum_columns(expansion_grad.reshape(dp_size, hidden_piece, width), 2, 1)
    mlp_input_grad = own_shape(
        sum_tokens([nn(rows, expansion_full) for rows in by_block(hidden_pre_grad)])
    )
    mid_part, shift_mlp_grad, scale_mlp_grad = mlp_pull(mlp_input_grad)
    mid_grad = out_grad + mid_part

    gate_attn_grad = jnp.sum(mid_grad * proj_out, axis=1)
    proj_out_grad = gather_tokens((gate_attn * mid_grad).astype(low).reshape(own_tokens, width))
    projection_grad = tn(proj_out_grad, attn_low).astype(low)
    attn_out_grad = to_heads(nn(proj_out_grad, projection_full).astype(low))
    delta = jnp.transpose(
        jnp.sum(attn_out_grad.astype(jnp.float32) * attn_out, axis=-1), (0, 2, 1)
    )
    scores = (
        jnp.einsum("lqhd,lkhd->lhqk", query, key, preferred_element_type=jnp.float32) * score_scale
    )
    probability = jnp.exp(scores - log_total[..., None])
    value_grad = jnp.einsum(
        "lhqk,lqhd->lkhd",
        probability.astype(low),
        attn_out_grad,
        preferred_element_type=jnp.float32,
    )
    prob_grad = jnp.einsum(
        "lqhd,lkhd->lhqk", attn_out_grad, value, preferred_element_type=jnp.float32
    )
    score_grad = (probability * (prob_grad - delta[..., None])).astype(low)
    query_grad = (
        jnp.einsum("lhqk,lkhd->lqhd", score_grad, key, preferred_element_type=jnp.float32)
        * score_scale
    )
    key_grad = (
        jnp.einsum("lhqk,lqhd->lkhd", score_grad, query, preferred_element_type=jnp.float32)
        * score_scale
    )
    qkv_grad = jnp.concatenate(
        [from_heads(grad.astype(low)) for grad in (query_grad, key_grad, value_grad)], axis=-1
    )
    attention_grad = tn(qkv_grad, attn_input).astype(low)
    attention_grad = attention_grad.reshape(3, own_width, seq_size, row_share)
    attention_grad = jnp.stack(in_order(around(by_distance(attention_grad, 2))), axis=1)
    small_grad = jnp.concatenate(
        [
            attention_grad.reshape(dp_size, qkv_share, row_share),
            projection_grad.reshape(dp_size, proj_share, row_share),
        ],
        axis=1,
    )
    small_sum = jnp.concatenate(
        [sum_columns(small_grad[:, :half], 1, 2), sum_columns(small_grad[:, half:], 2, 1)], axis=0
    ).astype(jnp.float32)
    attn_input_grad = own_shape(
        sum_tokens([nn(rows, attention_full) for rows in by_block(qkv_grad)])
    )
    resid_part, shift_attn_grad, scale_attn_grad = attn_pull(attn_input_grad)
    latent_grad = mid_grad + resid_part

    mod_grad = jnp.concatenate(
        [
            shift_attn_grad[:, 0, :],
            scale_attn_grad[:, 0, :],
            gate_attn_grad,
            shift_mlp_grad[:, 0, :],
            scale_mlp_grad[:, 0, :],
            gate_mlp_grad,
        ],
        axis=-1,
    )
    mod_grad = sum(around([mod_grad] * seq_size)).astype(low)
    mod_grad = jnp.transpose(mod_grad.reshape(local_latents, dp_size, mod_share), (1, 0, 2))
    mod_grad = lax.all_to_all(mod_grad, "dp", 0, 0, tiled=True).reshape(all_latents, mod_share)
    modulation_sum = tn(cond_rows, mod_grad)
    cond_part = nt(mod_grad, modulation_low).reshape(dp_size, local_latents * row_share)
    squares = jnp.broadcast_to(local_square, (dp_size, 128))
    back = lax.psum_scatter(
        jnp.concatenate([cond_part, squares], axis=1), "dp", scatter_dimension=0, tiled=True
    )
    back = jnp.stack(in_order(around([back] * seq_size)), axis=0)
    square_total = jnp.sum(back[:, 0, local_latents * row_share])
    masked_loss = square_total / (count_total * width)
    cond_grad = back[:, 0, : local_latents * row_share].reshape(seq_size, local_latents, row_share)
    cond_grad = jnp.transpose(cond_grad, (1, 0, 2)).reshape(local_latents, width)
    silu_pull = jax.vjp(silu_of, condition.astype(jnp.float32))[1]
    condition_grad = silu_pull(cond_grad)[0]

    expansion_sum = around(
        by_distance(expansion_sum.reshape(hidden_piece, seq_size, row_share), 1)
    )
    expansion_sum = jnp.concatenate(in_order(expansion_sum), axis=0).T
    contraction_sum = around(
        by_distance(
            contraction_sum.T.reshape(
                seq_size, dp_size // seq_size, hidden_piece, proj_share
            ),
            0,
        )
    )
    contraction_sum = jnp.stack(in_order(contraction_sum), axis=1).reshape(
        contraction_weight.shape
    )
    gradients = (
        modulation_sum,
        small_sum[:qkv_share].T,
        small_sum[qkv_share:].T,
        expansion_sum.astype(jnp.float32),
        contraction_sum.astype(jnp.float32),
    )

    step_rate = 0.06 / math.sqrt(all_latents * SEQ_LEN)
    masters = (
        modulation_weight,
        attention_weight,
        projection_weight,
        expansion_weight,
        contraction_weight,
    )
    moments = (
        modulation_moment,
        attention_moment,
        projection_moment,
        expansion_moment,
        contraction_moment,
    )
    averages = (
        modulation_average,
        attention_average,
        projection_average,
        expansion_average,
        contraction_average,
    )
    weight_next = []
    moment_next = []
    average_next = []
    for master, gradient, moment, average in zip(masters, gradients, moments, averages):
        moment_new = 0.5 * moment + gradient
        master_new = master - step_rate * (gradient + 0.5 * moment_new)
        weight_next.append(master_new)
        moment_next.append(moment_new)
        average_next.append(0.5 * average + 0.5 * master_new)
    return (
        block_output,
        masked_loss,
        latent_grad,
        condition_grad,
        *weight_next,
        *moment_next,
        *average_next,
    )


def solution(mesh):
    tokens_spec = P("dp", "seq", None)
    weight_spec = P("seq", "dp")
    in_specs = (
        tokens_spec,
        P("dp", None),
        tokens_spec,
        tokens_spec,
        P("dp", "seq"),
    ) + (weight_spec,) * 15
    out_specs = (tokens_spec, P(), tokens_spec, P("dp", None)) + (weight_spec,) * 15
    return jax.shard_map(body, mesh=mesh, in_specs=in_specs, out_specs=out_specs, check_vma=False)
```

```python
import math

import jax
import jax.numpy as jnp
from jax import lax
from jax.experimental import pallas as pl
from jax.experimental.pallas import tpu as pltpu
from jax.sharding import PartitionSpec as P

HEADS = 16
SEQ_LEN = 1024

epsilon = 1e-06
log2_e = math.log2(math.e)
low = jnp.bfloat16


def silu_of(values):
    return values * jax.nn.sigmoid(values)


def gelu_of(values):
    tanh_input = 0.7978845608028654 * (values + 0.044715 * values * values * values)
    return 0.5 * values * (1.0 + jnp.tanh(tanh_input))


def modulated(values, offset, stretch):
    centered = values - jnp.mean(values, axis=-1, keepdims=True)
    variance = jnp.mean(centered * centered, axis=-1, keepdims=True)
    return centered * lax.rsqrt(variance + epsilon) * (1.0 + stretch) + offset


def dot(first, second, over):
    return lax.dot_general(first, second, (over, ((), ())), preferred_element_type=jnp.float32)


def nn(first, second):
    return dot(first, second, ((1,), (0,)))


def nt(first, second):
    return dot(first, second, ((1,), (1,)))


def tn(first, second):
    return dot(first, second, ((0,), (0,)))


def around(pieces):
    size = lax.axis_size("seq")
    got = [pieces[0]] * size
    for r in range(1, size):
        steps = [(j, (j + r) % size) for j in range(size)]
        got[(size - r) % size] = lax.ppermute(pieces[r], "seq", steps)
    return got


def in_order(got):
    size = lax.axis_size("seq")
    me = lax.axis_index("seq")
    if size == 2:
        return [jnp.where(me == 0, got[0], got[1]), jnp.where(me == 0, got[1], got[0])]
    stacked = jnp.stack(got)
    return [lax.dynamic_index_in_dim(stacked, (j - me) % size, 0, False) for j in range(size)]


def by_distance(array, axis):
    size = lax.axis_size("seq")
    me = lax.axis_index("seq")
    return [lax.dynamic_index_in_dim(array, (me + r) % size, axis, False) for r in range(size)]


def gather_tokens(own):
    return jnp.concatenate(around([own] * lax.axis_size("seq")), axis=0)


def sum_tokens(parts):
    return sum(around(parts))


def swap(array, bit):
    size = lax.axis_size("dp")
    return lax.ppermute(array, "dp", [(j, j ^ bit) for j in range(size)])


def hypercube():
    size = lax.axis_size("dp")
    return size >= 4 and size & (size - 1) == 0


nothing = pl.CostEstimate(flops=0, bytes_accessed=0, transcendentals=0)
in_hbm = pl.BlockSpec(memory_space=pltpu.HBM)


def after(value, *others):
    def kernel(*refs):
        pass

    return pl.pallas_call(
        kernel,
        out_shape=jax.ShapeDtypeStruct(value.shape, value.dtype),
        in_specs=[in_hbm] * (1 + len(others)),
        out_specs=in_hbm,
        input_output_aliases={0: 0},
        cost_estimate=nothing,
    )(value, *others)


def place(pieces, distances):
    size = lax.axis_size("dp")
    index = jnp.array(distances, jnp.int32) ^ lax.axis_index("dp").astype(jnp.int32)
    each = size // len(pieces)

    def kernel(index_ref, *refs):
        sources, target = refs[: len(pieces)], refs[len(pieces)]
        held, arrived, left = refs[len(pieces) + 1 :]
        inward, outward = [], []
        for n in range(size):
            inward.append(
                pltpu.make_async_copy(sources[n // each].at[n % each], held.at[n], arrived.at[n])
            )
            inward[n].start()
        for n in range(size):
            inward[n].wait()
            outward.append(
                pltpu.make_async_copy(held.at[n], target.at[index_ref[n]], left.at[n])
            )
            outward[n].start()
        for n in range(size):
            outward[n].wait()

    whole = (size,) + pieces[0].shape[1:]
    return pl.pallas_call(
        kernel,
        out_shape=jax.ShapeDtypeStruct(whole, pieces[0].dtype),
        in_specs=[pl.BlockSpec(memory_space=pltpu.SMEM)] + [in_hbm] * len(pieces),
        out_specs=in_hbm,
        scratch_shapes=[
            pltpu.VMEM(whole, pieces[0].dtype),
            pltpu.SemaphoreType.DMA((size,)),
            pltpu.SemaphoreType.DMA((size,)),
        ],
        compiler_params=pltpu.CompilerParams(vmem_limit_bytes=24 << 20),
        cost_estimate=nothing,
    )(index, *pieces)


def gather_high(shard, *first):
    if not hypercube():
        return after(shard, *first) if first else shard, None
    held, distances = (after(shard, *first) if first else shard)[None], [0]
    bit = lax.axis_size("dp") >> 1
    while bit >= 4:
        held = jnp.concatenate([held, swap(held, bit)], axis=0)
        distances = distances + [d ^ bit for d in distances]
        bit >>= 1
    return held, distances


class Low:
    def __init__(self, high, first, last):
        self.held, self.high = high
        self.first, self.last = first, last
        if self.high is None:
            self.all = lax.all_gather(self.held, "dp", axis=0)

    def start(self):
        if self.high is not None:
            self.by_first = swap(self.held, self.first)
            self.by_last = swap(self.held, self.last)
        return self

    def step(self, *others):
        if self.high is not None:
            self.by_first = after(self.by_first, *others) if others else self.by_first
            self.by_both = swap(self.by_first, self.last)
        return self

    def middle(self):
        return [] if self.high is None else [self.by_first, self.by_last]

    def end(self):
        return [] if self.high is None else [self.by_both]

    def wait_for(self, *others):
        if self.high is not None and others:
            self.held = after(self.held, *others)
        return self

    def whole(self):
        if self.high is None:
            return self.all
        steps = (0, self.first, self.last, self.first | self.last)
        order = [d ^ step for step in steps for d in self.high]
        return place([self.held, self.by_first, self.by_last, self.by_both], order)


def plus(*parts):
    return sum(part.astype(jnp.float32) for part in parts).astype(parts[0].dtype)


class Sum:
    def __init__(self, blocks, first, last):
        self.blocks, self.first, self.last = blocks, first, last
        size = lax.axis_size("dp")
        if not hypercube():
            self.sent, self.onward, self.steps = [], [], []
            return
        me = lax.axis_index("dp")
        shape = blocks.shape[1:]
        split = blocks.reshape((size // 4, 2, 2) + shape)

        def group(distance):
            want = (me ^ distance) & 3
            part = lax.dynamic_slice(
                split, (0, want >> 1, want & 1) + (0,) * len(shape), (size // 4, 1, 1) + shape
            )
            return part.reshape((size // 4,) + shape)

        self.sent = [group(first | last), group(first)]
        far = swap(self.sent[0], first)
        near = swap(self.sent[1], first)
        self.onward = [plus(group(last), far)]
        self.kept, self.near, self.shape = group(0), near, shape

    def finish(self, *waits):
        if not hypercube():
            return lax.psum_scatter(self.blocks, "dp", scatter_dimension=0, tiled=False)
        waits = list(waits)

        def came(array):
            return after(array, *waits.pop(0)) if waits else array

        me = lax.axis_index("dp")
        onward = came(self.onward[0])
        held = plus(self.kept, self.near, came(swap(onward, self.last)))
        self.steps = [held]
        bit = 4
        while bit < lax.axis_size("dp"):
            pairs = held.reshape((held.shape[0] // 2, 2) + self.shape)
            mine = (me // bit) & 1
            away = lax.dynamic_index_in_dim(pairs, 1 - mine, 1, False)
            held = plus(lax.dynamic_index_in_dim(pairs, mine, 1, False), came(swap(away, bit)))
            bit <<= 1
        return held[0]


def gather_small(own, *others):
    size = lax.axis_size("dp")
    if not hypercube():
        return lax.all_gather(own, "dp", axis=0)
    me = lax.axis_index("dp")
    held, bit = own[None], 1
    while bit < size:
        came = swap(held, bit)
        upper = (me & bit) != 0
        held = jnp.concatenate(
            [jnp.where(upper, came, held), jnp.where(upper, held, came)], axis=0
        )
        bit <<= 1
        if bit == 4:
            held = after(held, *others)
    return held


def sum_small(blocks):
    return jnp.sum(lax.all_to_all(blocks, "dp", 0, 0, tiled=True), axis=0)


def softmax_kernel(heads, head_size, block, qkv_ref, out_ref, low_ref, log_ref, key_ref, value_ref):
    width, length = heads * head_size, qkv_ref.shape[1]
    for h in range(heads):
        cols = slice(h * head_size, (h + 1) * head_size)
        key_ref[...] = qkv_ref[0, :, width + h * head_size : width + (h + 1) * head_size]
        value_ref[...] = qkv_ref[0, :, 2 * width + h * head_size : 2 * width + (h + 1) * head_size]
        for b in range(length // block):
            rows = slice(b * block, (b + 1) * block)
            scores = nt(qkv_ref[0, rows, cols], key_ref[...]) * (head_size ** (-0.5) * log2_e)
            top = jnp.max(scores, axis=1, keepdims=True)
            raised = jnp.exp2(scores - top)
            total = jnp.sum(raised, axis=1, keepdims=True)
            out = nn(raised.astype(low), value_ref[...]) / total
            out_ref[0, rows, cols] = out
            low_ref[0, rows, cols] = out.astype(low)
            log_ref[0, h : h + 1, rows] = (top + jnp.log2(total)).T


def one_latent(*shape):
    return pl.BlockSpec((1,) + shape, lambda i: (i, 0, 0))


def attend(qkv, heads, head_size):
    latents, length, columns = qkv.shape
    width = heads * head_size
    return pl.pallas_call(
        lambda *refs: softmax_kernel(heads, head_size, math.gcd(length, 256), *refs),
        out_shape=(
            jax.ShapeDtypeStruct((latents, length, width), jnp.float32),
            jax.ShapeDtypeStruct((latents, length, width), low),
            jax.ShapeDtypeStruct((latents, heads, length), jnp.float32),
        ),
        grid=(latents,),
        in_specs=[one_latent(length, columns)],
        out_specs=(
            one_latent(length, width),
            one_latent(length, width),
            one_latent(heads, length),
        ),
        scratch_shapes=[pltpu.VMEM((length, head_size), low)] * 2,
        compiler_params=pltpu.CompilerParams(vmem_limit_bytes=48 << 20),
        cost_estimate=pl.CostEstimate(
            flops=4 * latents * length * length * width,
            bytes_accessed=10 * latents * heads * length * length,
            transcendentals=latents * heads * length * length,
        ),
    )(qkv)


def softmax_back_kernel(
    heads,
    head_size,
    block,
    qkv_ref,
    grad_ref,
    out_ref,
    log_ref,
    qkv_grad_ref,
    key_ref,
    value_ref,
    key_sum,
    value_sum,
):
    width, length = heads * head_size, qkv_ref.shape[1]
    scale = head_size ** (-0.5)
    for h in range(heads):
        cols = slice(h * head_size, (h + 1) * head_size)
        key_cols = slice(width + h * head_size, width + (h + 1) * head_size)
        value_cols = slice(2 * width + h * head_size, 2 * width + (h + 1) * head_size)
        key_ref[...] = qkv_ref[0, :, key_cols]
        value_ref[...] = qkv_ref[0, :, value_cols]
        for b in range(length // block):
            rows = slice(b * block, (b + 1) * block)
            query, grad = qkv_ref[0, rows, cols], grad_ref[0, rows, cols]
            delta = jnp.sum(
                (grad.astype(jnp.float32) * out_ref[0, rows, cols]).T, axis=0, keepdims=True
            )
            probability = jnp.exp2(
                nt(key_ref[...], query) * (scale * log2_e) - log_ref[0, h : h + 1, rows]
            )
            score_grad = (probability * (nt(value_ref[...], grad) - delta)).astype(low)
            key_part = nn(score_grad, query)
            value_part = nn(probability.astype(low), grad)
            key_sum[...] = key_part if b == 0 else key_sum[...] + key_part
            value_sum[...] = value_part if b == 0 else value_sum[...] + value_part
            qkv_grad_ref[0, rows, cols] = (tn(score_grad, key_ref[...]) * scale).astype(low)
        qkv_grad_ref[0, :, key_cols] = (key_sum[...] * scale).astype(low)
        qkv_grad_ref[0, :, value_cols] = value_sum[...].astype(low)


def attend_back(qkv, grad, out, log_total, heads, head_size):
    latents, length, columns = qkv.shape
    width = heads * head_size
    return pl.pallas_call(
        lambda *refs: softmax_back_kernel(heads, head_size, math.gcd(length, 512), *refs),
        out_shape=jax.ShapeDtypeStruct((latents, length, columns), low),
        grid=(latents,),
        in_specs=[
            one_latent(length, columns),
            one_latent(length, width),
            one_latent(length, width),
            one_latent(heads, length),
        ],
        out_specs=one_latent(length, columns),
        scratch_shapes=[pltpu.VMEM((length, head_size), low)] * 2
        + [pltpu.VMEM((length, head_size), jnp.float32)] * 2,
        compiler_params=pltpu.CompilerParams(vmem_limit_bytes=56 << 20),
        cost_estimate=pl.CostEstimate(
            flops=10 * latents * length * length * width,
            bytes_accessed=12 * latents * heads * length * length,
            transcendentals=latents * heads * length * length,
        ),
    )(qkv, grad, out, log_total)


def body(
    latents,
    condition,
    cotangent,
    teacher,
    valid_mask,
    modulation_weight,
    attention_weight,
    projection_weight,
    expansion_weight,
    contraction_weight,
    modulation_moment,
    attention_moment,
    projection_moment,
    expansion_moment,
    contraction_moment,
    modulation_average,
    attention_average,
    projection_average,
    expansion_average,
    contraction_average,
):
    local_latents, block_rows, width = latents.shape
    seq_size, dp_size = lax.axis_size("seq"), lax.axis_size("dp")
    seq_me, dp_me = lax.axis_index("seq"), lax.axis_index("dp")
    all_latents = local_latents * dp_size
    head_size = width // HEADS
    heads = HEADS // seq_size
    own_width = heads * head_size
    score_scale = head_size ** (-0.5)
    own_tokens = local_latents * block_rows
    tokens = own_tokens * seq_size
    row_share = attention_weight.shape[0]
    mod_share = modulation_weight.shape[1]
    qkv_share = attention_weight.shape[1]
    proj_share = projection_weight.shape[1]
    hidden_share = expansion_weight.shape[1]
    hidden_piece = hidden_share // seq_size

    attention_low = attention_weight.astype(low).T
    expansion_low = after(expansion_weight.astype(low).T, attention_low)
    expansion_low = expansion_low.reshape(seq_size, hidden_piece, row_share)
    expansion_shard = jnp.concatenate(in_order(around(by_distance(expansion_low, 0))), axis=1)
    contraction_low = after(contraction_weight.astype(low), attention_low).reshape(
        dp_size // seq_size, seq_size, hidden_piece, proj_share
    )
    contraction_shard = jnp.concatenate(in_order(around(by_distance(contraction_low, 1))), axis=0)
    contraction_shard = contraction_shard.reshape(dp_size * hidden_piece, proj_share).T
    projection_low = projection_weight.astype(low).T

    def widen(shard):
        rows, columns = shard.shape
        if columns >= width:
            return jnp.concatenate(jnp.split(shard, columns // width, axis=1), axis=0)
        return jnp.concatenate(jnp.split(shard, width // columns, axis=0), axis=1)

    def narrow(wide, rows):
        if wide.shape[-2] >= rows:
            return jnp.concatenate(jnp.split(wide, wide.shape[-2] // rows, axis=-2), axis=-1)
        return jnp.concatenate(jnp.split(wide, rows // wide.shape[-2], axis=-1), axis=-2)

    def widen_blocks(blocks):
        return jax.vmap(widen)(blocks)

    rides = width % own_width == 0 and proj_share % (width // own_width) == 0
    one = [widen(contraction_shard), expansion_shard]
    if rides:
        one.append(widen(projection_low))
    cut_c = one[0].shape[0]
    cut_e = cut_c + hidden_piece
    one_full = lax.all_gather(jnp.concatenate(one, axis=0), "dp", axis=0)
    if not rides:
        projection_full = lax.all_gather(projection_low, "dp", axis=0)

    attention_high = gather_high(attention_low)
    first_ready = [attention_high[0]]
    half = (qkv_share // 2 + 15) // 16 * 16

    def rows_of(high, rows):
        held, distances = high
        return (held[..., rows, :], distances)

    attention_a = Low(rows_of(attention_high, slice(0, half)), 1, 2).start().step()
    attention_b = Low(rows_of(attention_high, slice(half, None)), 2, 1).start().step()

    mask_float = valid_mask.astype(jnp.float32)
    chunk = math.gcd(own_tokens, 128)
    counts = jnp.sum(mask_float.reshape(own_tokens // chunk, chunk), axis=1).astype(low)
    packed = jnp.concatenate([condition.reshape(-1), counts])
    packed = gather_small(jnp.stack(in_order(around([packed] * seq_size))), *first_ready)
    count_total = jnp.sum(packed[:, :, local_latents * width :].astype(jnp.float32))
    every_cond = packed[:, 0, : local_latents * width].reshape(all_latents, width)
    cond_active = silu_of(every_cond.astype(jnp.float32)).astype(low)
    cond_rows = lax.dynamic_slice(
        cond_active, (0, seq_me * row_share), (all_latents, row_share)
    )
    attention_rows = jnp.concatenate([attention_a.whole(), attention_b.whole()], axis=1)
    attention_rows = attention_rows.reshape(3, seq_size, own_width, row_share)
    attention_full = jnp.concatenate(
        in_order(around(by_distance(attention_rows, 1))), axis=-1
    ).reshape(3 * own_width, width)

    modulation_low = modulation_weight.astype(low)
    mod_part = nn(cond_rows, modulation_low).reshape(dp_size, local_latents, mod_share)
    mod_part = lax.all_to_all(mod_part, "dp", 0, 0, tiled=True)
    modulation = sum(around([mod_part] * seq_size))
    modulation = jnp.transpose(modulation, (1, 0, 2)).reshape(local_latents, dp_size * mod_share)
    shift_attn, scale_attn, gate_attn, shift_mlp, scale_mlp, gate_mlp = [
        group[:, None, :] for group in jnp.split(modulation, 6, axis=-1)
    ]

    residual_in = latents.astype(jnp.float32)
    attn_value, attn_pull = jax.vjp(modulated, residual_in, shift_attn, scale_attn)
    attn_input = gather_tokens(attn_value.astype(low).reshape(own_tokens, width))
    qkv_low = nt(attn_input, attention_full).astype(low)

    def by_latent(array):
        array = array.reshape(seq_size, local_latents, block_rows, -1)
        return jnp.transpose(array, (1, 0, 2, 3)).reshape(
            local_latents, seq_size * block_rows, -1
        )

    def by_device(array):
        array = array.reshape(local_latents, seq_size, block_rows, -1)
        return jnp.transpose(array, (1, 0, 2, 3)).reshape(tokens, -1)

    qkv = by_latent(qkv_low)
    attn_out, attn_low, log_total = attend(qkv, heads, head_size)
    attn_low = by_device(attn_low)

    one_full = after(one_full, attn_low)
    contraction_full = narrow(one_full[:, :cut_c], proj_share).reshape(
        width, dp_size * hidden_piece
    )
    expansion_full = one_full[:, cut_c:cut_e].reshape(dp_size * hidden_piece, width)
    if rides:
        projection_full = narrow(one_full[:, cut_e:], proj_share)
    projection_full = projection_full.reshape(width, own_width)

    def by_block(array):
        return [array[r * own_tokens : (r + 1) * own_tokens] for r in range(seq_size)]

    def own_shape(array):
        return array.reshape(local_latents, block_rows, width)

    proj_out = own_shape(sum_tokens([nt(rows, projection_full) for rows in by_block(attn_low)]))
    mid_resid = residual_in + gate_attn * proj_out

    mlp_value, mlp_pull = jax.vjp(modulated, mid_resid, shift_mlp, scale_mlp)
    mlp_input = gather_tokens(mlp_value.astype(low).reshape(own_tokens, width))
    hidden_pre = nt(mlp_input, expansion_full)
    gelu_value, gelu_pull = jax.vjp(gelu_of, hidden_pre)
    hidden_low = gelu_value.astype(low)
    mlp_out = own_shape(sum_tokens([nt(rows, contraction_full) for rows in by_block(hidden_low)]))
    block_output = mid_resid + gate_mlp * mlp_out

    teacher_gap = block_output - teacher.astype(jnp.float32)
    local_square = jnp.sum(mask_float[..., None] * teacher_gap * teacher_gap)
    out_grad = cotangent.astype(jnp.float32) + 2.0 * mask_float[..., None] * teacher_gap / (
        count_total * width
    )

    gate_mlp_grad = jnp.sum(out_grad * mlp_out, axis=1)
    mlp_out_grad = gather_tokens((gate_mlp * out_grad).astype(low).reshape(own_tokens, width))
    folds = max(dp_size * hidden_piece // width, 1)
    contraction_grad = [
        tn(mlp_out_grad, part).astype(low).reshape(dp_size, proj_share, -1)
        for part in jnp.split(hidden_low, folds, axis=1)
    ]
    hidden_grad = nn(mlp_out_grad, contraction_full)
    hidden_pre_grad = gelu_pull(hidden_grad)[0].astype(low)
    expansion_grad = tn(hidden_pre_grad, mlp_input).astype(low)
    expansion_grad = expansion_grad.reshape(dp_size, hidden_piece, width)
    if contraction_grad[0].shape[-1] != width:
        contraction_grad = [widen_blocks(part) for part in contraction_grad]
    mlp_sum = lax.psum_scatter(
        jnp.concatenate(contraction_grad + [expansion_grad], axis=1),
        "dp",
        scatter_dimension=0,
        tiled=False,
    )
    contraction_sum = narrow(mlp_sum[:cut_c], proj_share)
    expansion_sum = mlp_sum[cut_c:]
    mlp_input_grad = own_shape(
        sum_tokens([nn(rows, expansion_full) for rows in by_block(hidden_pre_grad)])
    )
    mid_part, shift_mlp_grad, scale_mlp_grad = mlp_pull(mlp_input_grad)
    mid_grad = out_grad + mid_part

    gate_attn_grad = jnp.sum(mid_grad * proj_out, axis=1)
    proj_out_grad = gather_tokens((gate_attn * mid_grad).astype(low).reshape(own_tokens, width))
    projection_grad = tn(proj_out_grad, attn_low).astype(low)
    attn_out_grad = by_latent(nn(proj_out_grad, projection_full).astype(low))
    qkv_grad = by_device(
        attend_back(qkv, attn_out_grad, attn_out, log_total, heads, head_size)
    )
    features = attn_input.reshape(tokens, seq_size, row_share)
    attention_grad = [
        tn(qkv_grad, columns).astype(low).reshape(3, own_width, row_share)
        for columns in by_distance(features, 1)
    ]
    attention_grad = jnp.stack(in_order(around(attention_grad)), axis=1).reshape(
        dp_size, qkv_share, row_share
    )
    small_grad = jnp.concatenate(
        [attention_grad, projection_grad.reshape(dp_size, proj_share, own_width)], axis=1
    )
    small_half = small_grad.shape[1] // 2
    attention_sum = [
        Sum(small_grad[:, :small_half], 1, 2),
        Sum(small_grad[:, small_half:], 2, 1),
    ]
    qkv_grad = after(qkv_grad, *attention_sum[0].sent, *attention_sum[1].sent)
    attn_input_grad = own_shape(
        sum_tokens([nn(rows, attention_full) for rows in by_block(qkv_grad)])
    )
    resid_part, shift_attn_grad, scale_attn_grad = attn_pull(attn_input_grad)
    latent_grad = mid_grad + resid_part

    mod_grad = jnp.concatenate(
        [
            shift_attn_grad[:, 0, :],
            scale_attn_grad[:, 0, :],
            gate_attn_grad,
            shift_mlp_grad[:, 0, :],
            scale_mlp_grad[:, 0, :],
            gate_mlp_grad,
        ],
        axis=-1,
    )
    mod_local = mod_grad
    mod_grad = sum(around([mod_grad] * seq_size)).astype(low)
    mod_grad = jnp.transpose(mod_grad.reshape(local_latents, dp_size, mod_share), (1, 0, 2))
    mod_grad = lax.all_to_all(mod_grad, "dp", 0, 0, tiled=True).reshape(all_latents, mod_share)
    modulation_sum = tn(cond_rows, mod_grad)
    cond_part = nt(mod_grad, modulation_low).reshape(dp_size, local_latents * row_share)
    squares = jnp.broadcast_to(local_square, (dp_size, 128))
    back = sum_small(jnp.concatenate([cond_part, squares], axis=1))[None]
    back = jnp.stack(in_order(around([back] * seq_size)), axis=0)
    square_total = jnp.sum(back[:, 0, local_latents * row_share])
    masked_loss = square_total / (count_total * width)
    cond_grad = back[:, 0, : local_latents * row_share].reshape(seq_size, local_latents, row_share)
    cond_grad = jnp.transpose(cond_grad, (1, 0, 2)).reshape(local_latents, width)
    silu_pull = jax.vjp(silu_of, condition.astype(jnp.float32))[1]
    condition_grad = silu_pull(cond_grad)[0]

    waits = [mod_local], [cond_part], [back]
    attention_sum = jnp.concatenate([part.finish(*waits) for part in attention_sum], axis=0)
    expansion_sum = around(
        by_distance(expansion_sum.reshape(hidden_piece, seq_size, row_share), 1)
    )
    expansion_sum = jnp.concatenate(in_order(expansion_sum), axis=0).T
    contraction_sum = around(
        by_distance(
            contraction_sum.T.reshape(
                seq_size, dp_size // seq_size, hidden_piece, proj_share
            ),
            0,
        )
    )
    contraction_sum = jnp.stack(in_order(contraction_sum), axis=1).reshape(
        contraction_weight.shape
    )
    gradients = (
        modulation_sum,
        attention_sum[:qkv_share].astype(jnp.float32).T,
        attention_sum[qkv_share:].astype(jnp.float32).T,
        expansion_sum.astype(jnp.float32),
        contraction_sum.astype(jnp.float32),
    )

    step_rate = 0.06 / math.sqrt(all_latents * SEQ_LEN)
    masters = (
        modulation_weight,
        attention_weight,
        projection_weight,
        expansion_weight,
        contraction_weight,
    )
    moments = (
        modulation_moment,
        attention_moment,
        projection_moment,
        expansion_moment,
        contraction_moment,
    )
    averages = (
        modulation_average,
        attention_average,
        projection_average,
        expansion_average,
        contraction_average,
    )
    weight_next = []
    moment_next = []
    average_next = []
    for master, gradient, moment, average in zip(masters, gradients, moments, averages):
        moment_new = 0.5 * moment + gradient
        master_new = master - step_rate * (gradient + 0.5 * moment_new)
        weight_next.append(master_new)
        moment_next.append(moment_new)
        average_next.append(0.5 * average + 0.5 * master_new)
    return (
        block_output,
        masked_loss,
        latent_grad,
        condition_grad,
        *weight_next,
        *moment_next,
        *average_next,
    )


def solution(mesh):
    tokens_spec = P("dp", "seq", None)
    weight_spec = P("seq", "dp")
    in_specs = (
        tokens_spec,
        P("dp", None),
        tokens_spec,
        tokens_spec,
        P("dp", "seq"),
    ) + (weight_spec,) * 15
    out_specs = (tokens_spec, P(), tokens_spec, P("dp", None)) + (weight_spec,) * 15
    return jax.shard_map(body, mesh=mesh, in_specs=in_specs, out_specs=out_specs, check_vma=False)
```

```python
import math

import jax
import jax.numpy as jnp
from jax import lax
from jax.experimental import pallas as pl
from jax.experimental.pallas import tpu as pltpu
from jax.sharding import PartitionSpec as P

HEADS = 16
SEQ_LEN = 1024

epsilon = 1e-06
log2_e = math.log2(math.e)
low = jnp.bfloat16


def silu_of(values):
    return values * jax.nn.sigmoid(values)


def gelu_of(values):
    square = values * values
    tanh = jnp.tanh(values * (0.7978845608028654 + (0.044715 * 0.7978845608028654) * square))
    half = 0.5 * tanh + 0.5
    value = values * half
    inner = 2 * 0.7978845608028654 + (6 * 0.044715 * 0.7978845608028654) * square
    return value, half + (value - value * half) * inner


def modulated(values, offset, stretch):
    centered = values - jnp.mean(values, axis=-1, keepdims=True)
    variance = jnp.mean(centered * centered, axis=-1, keepdims=True)
    return centered * lax.rsqrt(variance + epsilon) * (1.0 + stretch) + offset


def dot(first, second, over):
    return lax.dot_general(first, second, (over, ((), ())), preferred_element_type=jnp.float32)


def nn(first, second):
    return dot(first, second, ((1,), (0,)))


def nt(first, second):
    return dot(first, second, ((1,), (1,)))


def tn(first, second):
    return dot(first, second, ((0,), (0,)))


def around(pieces):
    size = lax.axis_size("seq")
    got = [pieces[0]] * size
    for r in range(1, size):
        steps = [(j, (j + r) % size) for j in range(size)]
        got[(size - r) % size] = lax.ppermute(pieces[r], "seq", steps)
    return got


def in_order(got):
    size = lax.axis_size("seq")
    me = lax.axis_index("seq")
    if size == 2:
        return [jnp.where(me == 0, got[0], got[1]), jnp.where(me == 0, got[1], got[0])]
    stacked = jnp.stack(got)
    return [lax.dynamic_index_in_dim(stacked, (j - me) % size, 0, False) for j in range(size)]


def by_distance(array, axis):
    size = lax.axis_size("seq")
    me = lax.axis_index("seq")
    return [lax.dynamic_index_in_dim(array, (me + r) % size, axis, False) for r in range(size)]


def gather_tokens(own):
    return lax.optimization_barrier(
        jnp.concatenate(around([own] * lax.axis_size("seq")), axis=0)
    )


def sum_tokens(parts):
    got = around(parts[:1] + [lax.optimization_barrier(part) for part in parts[1:]])
    return sum([lax.optimization_barrier(got[0])] + got[1:])


def swap(array, bit):
    size = lax.axis_size("dp")
    return lax.ppermute(array, "dp", [(j, j ^ bit) for j in range(size)])


def hypercube():
    size = lax.axis_size("dp")
    return size >= 4 and size & (size - 1) == 0


nothing = pl.CostEstimate(flops=0, bytes_accessed=0, transcendentals=0)
in_hbm = pl.BlockSpec(memory_space=pltpu.HBM)


def after(value, *others):
    def kernel(*refs):
        pass

    if not others:
        return value
    return pl.pallas_call(
        kernel,
        out_shape=jax.ShapeDtypeStruct(value.shape, value.dtype),
        in_specs=[in_hbm] * (1 + len(others)),
        out_specs=in_hbm,
        input_output_aliases={0: 0},
        cost_estimate=nothing,
    )(value, *others)


def place(*ways):
    size = lax.axis_size("dp")
    count = len(ways)
    me = lax.axis_index("dp").astype(jnp.int32)
    index = (jnp.array([steps for _, steps in ways], jnp.int32) ^ me) & 3

    def kernel(index_ref, *refs):
        sources, targets = refs[: 4 * count], refs[4 * count : 5 * count]
        held, (arrived, left) = refs[5 * count : 6 * count], refs[6 * count :]
        inward, outward = [], []
        for n in range(4):
            for w in range(count):
                copy = pltpu.make_async_copy(sources[4 * w + n], held[w].at[n], arrived.at[w, n])
                copy.start()
                inward.append(copy)
        for n in range(4):
            for w in range(count):
                inward[n * count + w].wait()
                target = targets[w].at[:, index_ref[w, n]]
                copy = pltpu.make_async_copy(held[w].at[n], target, left.at[w, n])
                copy.start()
                outward.append(copy)
        for copy in outward:
            copy.wait()

    groups = [pieces[0].shape for pieces, _ in ways]
    placed = pl.pallas_call(
        kernel,
        out_shape=[jax.ShapeDtypeStruct((g[0], 4) + g[1:], low) for g in groups],
        in_specs=[pl.BlockSpec(memory_space=pltpu.SMEM)] + [in_hbm] * (4 * count),
        out_specs=[in_hbm] * count,
        scratch_shapes=[pltpu.VMEM((4,) + g, low) for g in groups]
        + [pltpu.SemaphoreType.DMA((count, 4))] * 2,
        compiler_params=pltpu.CompilerParams(vmem_limit_bytes=24 << 20),
        cost_estimate=nothing,
    )(index, *[piece for pieces, _ in ways for piece in pieces])
    return [whole.reshape((size,) + whole.shape[2:]) for whole in placed]


def gather_high(shard):
    if not hypercube():
        return shard
    held, bit = shard[None], lax.axis_size("dp") >> 1
    while bit >= 4:
        came = swap(held, bit)
        upper = (lax.axis_index("dp") & bit) != 0
        pair = [jnp.where(upper, came, held), jnp.where(upper, held, came)]
        held = jnp.stack(pair, axis=1).reshape((-1,) + held.shape[1:])
        bit >>= 1
    return held


class Low:
    def __init__(self, held, first, last):
        self.held, self.first, self.last = held, first, last
        if not hypercube():
            self.all = lax.all_gather(held, "dp", axis=0)
            return
        self.by_first = swap(held, first)
        self.by_last = swap(held, last)
        self.by_both = swap(self.by_first, last)

    def pieces(self):
        steps = (0, self.first, self.last, self.first | self.last)
        return [self.held, self.by_first, self.by_last, self.by_both], steps


def wholes(*ways):
    if not hypercube():
        return [way.all for way in ways]
    return place(*[way.pieces() for way in ways])


def plus(*parts):
    return sum(part.astype(jnp.float32) for part in parts).astype(parts[0].dtype)


class Sum:
    def __init__(self, blocks, first, last):
        self.blocks, self.first, self.last = blocks, first, last
        size = lax.axis_size("dp")
        if not hypercube():
            self.sent = []
            return
        me = lax.axis_index("dp")

        def group(distance):
            want = (me ^ distance) & 3
            parts = []
            for block in blocks:
                shape = block.shape[1:]
                part = lax.dynamic_slice(
                    block.reshape((size // 4, 2, 2) + shape),
                    (0, want >> 1, want & 1) + (0,) * len(shape),
                    (size // 4, 1, 1) + shape,
                )
                parts.append(part.reshape((size // 4,) + shape))
            return jnp.concatenate(parts, axis=1)

        self.sent = [group(first | last), group(first)]
        self.far = swap(self.sent[0], first)
        self.near = swap(self.sent[1], first)
        self.kept = group(last), group(0)

    def second(self, *others):
        self.passed = []
        if hypercube():
            self.onward = plus(self.kept[0], after(self.far, *others))
            self.passed = [self.onward]

    def third(self, *others):
        self.held = []
        if hypercube():
            through = swap(after(self.onward, *others), self.last)
            self.total = plus(self.kept[1], self.near, through)
            self.held = [self.total]

    def finish(self, *waits):
        if not hypercube():
            blocks = jnp.concatenate(self.blocks, axis=1)
            return lax.psum_scatter(blocks, "dp", scatter_dimension=0, tiled=False)
        waits = list(waits)

        def came(array):
            return after(array, *waits.pop(0)) if waits else array

        me = lax.axis_index("dp")
        held, bit = self.total, 4
        while bit < lax.axis_size("dp"):
            pairs = held.reshape((held.shape[0] // 2, 2) + held.shape[1:])
            mine = (me // bit) & 1
            away = lax.dynamic_index_in_dim(pairs, 1 - mine, 1, False)
            held = plus(lax.dynamic_index_in_dim(pairs, mine, 1, False), came(swap(away, bit)))
            bit <<= 1
        return held[0]


def gather_small(own, *others):
    size = lax.axis_size("dp")
    if not hypercube():
        return lax.all_gather(own, "dp", axis=0)
    me = lax.axis_index("dp")
    held, bit = own[None], 1
    while bit < size:
        came = swap(held, bit)
        upper = (me & bit) != 0
        held = jnp.concatenate(
            [jnp.where(upper, came, held), jnp.where(upper, held, came)], axis=0
        )
        bit <<= 1
        if bit == 4:
            held = after(held, *others)
    return held


def sum_small(blocks):
    return jnp.sum(lax.all_to_all(blocks, "dp", 0, 0, tiled=True), axis=0)


def softmax_kernel(heads, head_size, block, qkv_ref, out_ref, low_ref, log_ref, key_ref, value_ref):
    width, length = heads * head_size, qkv_ref.shape[1]
    for h in range(heads):
        cols = slice(h * head_size, (h + 1) * head_size)
        key_ref[...] = qkv_ref[0, :, width + h * head_size : width + (h + 1) * head_size]
        value_ref[...] = qkv_ref[0, :, 2 * width + h * head_size : 2 * width + (h + 1) * head_size]
        for b in range(length // block):
            rows = slice(b * block, (b + 1) * block)
            scores = nt(qkv_ref[0, rows, cols], key_ref[...]) * (head_size ** (-0.5) * log2_e)
            top = jnp.max(scores, axis=1, keepdims=True)
            raised = jnp.exp2(scores - top)
            total = jnp.sum(raised, axis=1, keepdims=True)
            out = nn(raised.astype(low), value_ref[...]) / total
            out_ref[0, rows, cols] = out
            low_ref[0, rows, cols] = out.astype(low)
            log_ref[0, h : h + 1, rows] = (top + jnp.log2(total)).T


def one_latent(*shape):
    return pl.BlockSpec((1,) + shape, lambda i: (i, 0, 0))


def attend(qkv, heads, head_size):
    latents, length, columns = qkv.shape
    width = heads * head_size
    return pl.pallas_call(
        lambda *refs: softmax_kernel(heads, head_size, math.gcd(length, 256), *refs),
        out_shape=(
            jax.ShapeDtypeStruct((latents, length, width), jnp.float32),
            jax.ShapeDtypeStruct((latents, length, width), low),
            jax.ShapeDtypeStruct((latents, heads, length), jnp.float32),
        ),
        grid=(latents,),
        in_specs=[one_latent(length, columns)],
        out_specs=(
            one_latent(length, width),
            one_latent(length, width),
            one_latent(heads, length),
        ),
        scratch_shapes=[pltpu.VMEM((length, head_size), low)] * 2,
        compiler_params=pltpu.CompilerParams(vmem_limit_bytes=48 << 20),
        cost_estimate=pl.CostEstimate(
            flops=4 * latents * length * length * width,
            bytes_accessed=10 * latents * heads * length * length,
            transcendentals=latents * heads * length * length,
        ),
    )(qkv)


def softmax_back_kernel(
    heads,
    head_size,
    block,
    qkv_ref,
    grad_ref,
    out_ref,
    log_ref,
    qkv_grad_ref,
    key_ref,
    value_ref,
    key_sum,
    value_sum,
):
    width, length = heads * head_size, qkv_ref.shape[1]
    scale = head_size ** (-0.5)
    for h in range(heads):
        cols = slice(h * head_size, (h + 1) * head_size)
        key_cols = slice(width + h * head_size, width + (h + 1) * head_size)
        value_cols = slice(2 * width + h * head_size, 2 * width + (h + 1) * head_size)
        key_ref[...] = qkv_ref[0, :, key_cols]
        value_ref[...] = qkv_ref[0, :, value_cols]
        for b in range(length // block):
            rows = slice(b * block, (b + 1) * block)
            query, grad = qkv_ref[0, rows, cols], grad_ref[0, rows, cols]
            delta = jnp.sum(
                (grad.astype(jnp.float32) * out_ref[0, rows, cols]).T, axis=0, keepdims=True
            )
            probability = jnp.exp2(
                nt(key_ref[...], query) * (scale * log2_e) - log_ref[0, h : h + 1, rows]
            )
            score_grad = (probability * (nt(value_ref[...], grad) - delta)).astype(low)
            key_part = nn(score_grad, query)
            value_part = nn(probability.astype(low), grad)
            key_sum[...] = key_part if b == 0 else key_sum[...] + key_part
            value_sum[...] = value_part if b == 0 else value_sum[...] + value_part
            qkv_grad_ref[0, rows, cols] = (tn(score_grad, key_ref[...]) * scale).astype(low)
        qkv_grad_ref[0, :, key_cols] = (key_sum[...] * scale).astype(low)
        qkv_grad_ref[0, :, value_cols] = value_sum[...].astype(low)


def attend_back(qkv, grad, out, log_total, heads, head_size):
    latents, length, columns = qkv.shape
    width = heads * head_size
    return pl.pallas_call(
        lambda *refs: softmax_back_kernel(heads, head_size, math.gcd(length, 512), *refs),
        out_shape=jax.ShapeDtypeStruct((latents, length, columns), low),
        grid=(latents,),
        in_specs=[
            one_latent(length, columns),
            one_latent(length, width),
            one_latent(length, width),
            one_latent(heads, length),
        ],
        out_specs=one_latent(length, columns),
        scratch_shapes=[pltpu.VMEM((length, head_size), low)] * 2
        + [pltpu.VMEM((length, head_size), jnp.float32)] * 2,
        compiler_params=pltpu.CompilerParams(vmem_limit_bytes=56 << 20),
        cost_estimate=nothing,
    )(qkv, grad, out, log_total)


def body(
    latents,
    condition,
    cotangent,
    teacher,
    valid_mask,
    modulation_weight,
    attention_weight,
    projection_weight,
    expansion_weight,
    contraction_weight,
    modulation_moment,
    attention_moment,
    projection_moment,
    expansion_moment,
    contraction_moment,
    modulation_average,
    attention_average,
    projection_average,
    expansion_average,
    contraction_average,
):
    local_latents, block_rows, width = latents.shape
    seq_size, dp_size = lax.axis_size("seq"), lax.axis_size("dp")
    seq_me, dp_me = lax.axis_index("seq"), lax.axis_index("dp")
    all_latents = local_latents * dp_size
    head_size = width // HEADS
    heads = HEADS // seq_size
    own_width = heads * head_size
    score_scale = head_size ** (-0.5)
    own_tokens = local_latents * block_rows
    tokens = own_tokens * seq_size
    row_share = attention_weight.shape[0]
    mod_share = modulation_weight.shape[1]
    qkv_share = attention_weight.shape[1]
    proj_share = projection_weight.shape[1]
    hidden_share = expansion_weight.shape[1]
    hidden_piece = hidden_share // seq_size

    row_room = (row_share + 127) // 128 * 128

    def roomy(array):
        return jnp.pad(array, [(0, 0)] * (array.ndim - 1) + [(0, row_room - array.shape[-1])])

    attention_low = roomy(attention_weight.astype(low).T)
    expansion_low = after(expansion_weight.astype(low).T, attention_low)
    expansion_low = expansion_low.reshape(seq_size, hidden_piece, row_share)
    expansion_shard = jnp.concatenate(in_order(around(by_distance(expansion_low, 0))), axis=1)
    contraction_low = after(contraction_weight.astype(low), attention_low).reshape(
        dp_size // seq_size, seq_size, hidden_piece, proj_share
    )
    contraction_shard = jnp.concatenate(in_order(around(by_distance(contraction_low, 1))), axis=0)
    contraction_shard = contraction_shard.reshape(dp_size * hidden_piece, proj_share).T
    projection_low = projection_weight.astype(low).T

    def widen(shard):
        rows, columns = shard.shape
        if columns >= width:
            return jnp.concatenate(jnp.split(shard, columns // width, axis=1), axis=0)
        return jnp.concatenate(jnp.split(shard, width // columns, axis=0), axis=1)

    def narrow(wide, rows):
        if wide.shape[-2] >= rows:
            return jnp.concatenate(jnp.split(wide, wide.shape[-2] // rows, axis=-2), axis=-1)
        return jnp.concatenate(jnp.split(wide, rows // wide.shape[-2], axis=-1), axis=-2)

    def widen_blocks(blocks):
        return jax.vmap(widen)(blocks)

    rides = width % own_width == 0 and proj_share % (width // own_width) == 0
    one = [widen(contraction_shard), expansion_shard]
    if rides:
        one.append(widen(projection_low))
    cut_c = one[0].shape[0]
    cut_e = cut_c + hidden_piece
    one_full = lax.all_gather(jnp.concatenate(one, axis=0), "dp", axis=0)
    if not rides:
        projection_full = lax.all_gather(projection_low, "dp", axis=0)

    attention_high = gather_high(attention_low)
    first_ready = [attention_high]
    half = (qkv_share // 2 + 15) // 16 * 16
    attention_a = Low(attention_high[..., :half, :], 1, 2)
    attention_b = Low(attention_high[..., half:, :], 2, 1)

    mask_float = valid_mask.astype(jnp.float32)
    chunk = math.gcd(own_tokens, 128)
    counts = jnp.sum(mask_float.reshape(own_tokens // chunk, chunk), axis=1).astype(low)
    packed = jnp.concatenate([condition.reshape(-1), counts])
    packed = gather_small(jnp.stack(in_order(around([packed] * seq_size))), *first_ready)
    count_total = jnp.sum(packed[:, :, local_latents * width :].astype(jnp.float32))
    every_cond = packed[:, 0, : local_latents * width].reshape(all_latents, width)
    cond_active = silu_of(every_cond.astype(jnp.float32)).astype(low)
    cond_rows = lax.dynamic_slice(
        cond_active, (0, seq_me * row_share), (all_latents, row_share)
    )
    attention_rows = jnp.concatenate(wholes(attention_a, attention_b), axis=1)
    attention_rows = attention_rows.reshape(3, seq_size, own_width, row_room)
    attention_full = jnp.concatenate(
        in_order(around(by_distance(attention_rows, 1))), axis=-1
    ).reshape(3 * own_width, seq_size * row_room)

    modulation_low = modulation_weight.astype(low)
    mod_part = nn(cond_rows, modulation_low).reshape(dp_size, local_latents, mod_share)
    mod_part = lax.all_to_all(mod_part, "dp", 0, 0, tiled=True)
    modulation = sum(around([mod_part] * seq_size))
    modulation = jnp.transpose(modulation, (1, 0, 2)).reshape(local_latents, dp_size * mod_share)
    shift_attn, scale_attn, gate_attn, shift_mlp, scale_mlp, gate_mlp = [
        group[:, None, :] for group in jnp.split(modulation, 6, axis=-1)
    ]

    residual_in = latents.astype(jnp.float32)
    attn_value, attn_pull = jax.vjp(modulated, residual_in, shift_attn, scale_attn)
    attn_input = roomy(attn_value.astype(low).reshape(own_tokens, seq_size, row_share))
    attn_input = gather_tokens(attn_input.reshape(own_tokens, seq_size * row_room))
    qkv_low = nt(attn_input, attention_full).astype(low)

    def by_latent(array):
        array = array.reshape(seq_size, local_latents, block_rows, -1)
        return jnp.transpose(array, (1, 0, 2, 3)).reshape(
            local_latents, seq_size * block_rows, -1
        )

    def by_device(array):
        array = array.reshape(local_latents, seq_size, block_rows, -1)
        return jnp.transpose(array, (1, 0, 2, 3)).reshape(tokens, -1)

    qkv = by_latent(qkv_low)
    attn_out, attn_low, log_total = attend(qkv, heads, head_size)
    attn_low = by_device(attn_low)

    one_full = after(one_full, attn_low)
    contraction_full = narrow(one_full[:, :cut_c], proj_share).reshape(
        width, dp_size * hidden_piece
    )
    expansion_full = one_full[:, cut_c:cut_e].reshape(dp_size * hidden_piece, width)
    if rides:
        projection_full = narrow(one_full[:, cut_e:], proj_share)
    projection_full = projection_full.reshape(width, own_width)

    def by_block(array):
        return [array[r * own_tokens : (r + 1) * own_tokens] for r in range(seq_size)]

    def own_shape(array):
        return array.reshape(local_latents, block_rows, width)

    proj_out = own_shape(sum_tokens([nt(rows, projection_full) for rows in by_block(attn_low)]))
    mid_resid = residual_in + gate_attn * proj_out

    mlp_value, mlp_pull = jax.vjp(modulated, mid_resid, shift_mlp, scale_mlp)
    mlp_input = gather_tokens(mlp_value.astype(low).reshape(own_tokens, width))
    value, slope = gelu_of(nt(mlp_input, expansion_full))
    hidden_low, hidden_slope = lax.optimization_barrier((value.astype(low), slope.astype(low)))
    mlp_out = own_shape(sum_tokens([nt(rows, contraction_full) for rows in by_block(hidden_low)]))
    block_output = mid_resid + gate_mlp * mlp_out

    teacher_gap = block_output - teacher.astype(jnp.float32)
    local_square = jnp.sum(mask_float[..., None] * teacher_gap * teacher_gap)
    out_grad = cotangent.astype(jnp.float32) + 2.0 * mask_float[..., None] * teacher_gap / (
        count_total * width
    )

    gate_mlp_grad = jnp.sum(out_grad * mlp_out, axis=1)
    mlp_out_grad = gather_tokens((gate_mlp * out_grad).astype(low).reshape(own_tokens, width))
    folds = max(dp_size * hidden_piece // width, 1)
    contraction_grad = [
        tn(mlp_out_grad, part).astype(low).reshape(dp_size, proj_share, -1)
        for part in jnp.split(hidden_low, folds, axis=1)
    ]
    hidden_grad = nn(mlp_out_grad, contraction_full)
    hidden_pre_grad = (hidden_grad * hidden_slope.astype(jnp.float32)).astype(low)
    expansion_grad = tn(hidden_pre_grad, mlp_input).astype(low)
    expansion_grad = expansion_grad.reshape(dp_size, hidden_piece, width)
    if contraction_grad[0].shape[-1] != width:
        contraction_grad = [widen_blocks(part) for part in contraction_grad]
    mlp_grads = jnp.concatenate(contraction_grad + [expansion_grad], axis=1)
    expansion_back = after(expansion_full, mlp_grads)
    mlp_sum = lax.psum_scatter(mlp_grads, "dp", scatter_dimension=0, tiled=False)
    if cut_c == seq_size * proj_share:
        contraction_sum = by_distance(mlp_sum[:cut_c].reshape(seq_size, proj_share, width), 0)
    else:
        contraction_sum = narrow(mlp_sum[:cut_c], proj_share).reshape(proj_share, seq_size, -1)
        contraction_sum = by_distance(contraction_sum, 1)
    expansion_sum = mlp_sum[cut_c:]
    mlp_input_grad = own_shape(
        sum_tokens([nn(rows, expansion_back) for rows in by_block(hidden_pre_grad)])
    )
    mid_part, shift_mlp_grad, scale_mlp_grad = mlp_pull(mlp_input_grad)
    mid_grad = out_grad + mid_part

    gate_attn_grad = jnp.sum(mid_grad * proj_out, axis=1)
    proj_out_grad = gather_tokens((gate_attn * mid_grad).astype(low).reshape(own_tokens, width))
    projection_grad = tn(proj_out_grad, roomy(attn_low)).astype(low)
    attn_out_grad = by_latent(nn(proj_out_grad, projection_full).astype(low))
    qkv_grad = by_device(
        attend_back(qkv, attn_out_grad, attn_out, log_total, heads, head_size)
    )
    features = attn_input.reshape(tokens, seq_size, row_room)
    attention_grad = [
        tn(qkv_grad, columns).astype(low).reshape(3, own_width, row_room)
        for columns in by_distance(features, 1)
    ]
    attention_grad = jnp.stack(in_order(around(attention_grad)), axis=1).reshape(
        dp_size, qkv_share, row_room
    )
    projection_grad = projection_grad.reshape(dp_size, proj_share, row_room)
    sum_half = (qkv_share + proj_share) // 2
    attention_sum = [
        Sum([attention_grad[:, :sum_half]], 1, 2),
        Sum([attention_grad[:, sum_half:], projection_grad], 2, 1),
    ]
    qkv_grad = after(qkv_grad, *attention_sum[0].sent, *attention_sum[1].sent)
    attn_input_grad = sum_tokens([nn(rows, attention_full) for rows in by_block(qkv_grad)])
    attn_input_grad = attn_input_grad.reshape(own_tokens, seq_size, row_room)[..., :row_share]
    attn_input_grad = own_shape(attn_input_grad)
    resid_part, shift_attn_grad, scale_attn_grad = attn_pull(attn_input_grad)
    latent_grad = mid_grad + resid_part

    mod_grad = jnp.concatenate(
        [
            shift_attn_grad[:, 0, :],
            scale_attn_grad[:, 0, :],
            gate_attn_grad,
            shift_mlp_grad[:, 0, :],
            scale_mlp_grad[:, 0, :],
            gate_mlp_grad,
        ],
        axis=-1,
    )
    mod_local = mod_grad
    mod_grad = sum(around([mod_grad] * seq_size)).astype(low)
    mod_grad = jnp.transpose(mod_grad.reshape(local_latents, dp_size, mod_share), (1, 0, 2))
    mod_grad = lax.all_to_all(mod_grad, "dp", 0, 0, tiled=True).reshape(all_latents, mod_share)
    for part in attention_sum:
        part.second(mod_local)
    for part in attention_sum:
        part.third(mod_grad)
    modulation_sum = tn(cond_rows, mod_grad)
    cond_part = nt(mod_grad, modulation_low).reshape(dp_size, local_latents * row_share)
    squares = jnp.broadcast_to(local_square, (dp_size, 128))
    back = sum_small(jnp.concatenate([cond_part, squares], axis=1))[None]
    back = after(back, *attention_sum[0].held, *attention_sum[1].held)
    back = jnp.stack(in_order(around([back] * seq_size)), axis=0)
    square_total = jnp.sum(back[:, 0, local_latents * row_share])
    masked_loss = square_total / (count_total * width)
    cond_grad = back[:, 0, : local_latents * row_share].reshape(seq_size, local_latents, row_share)
    cond_grad = jnp.transpose(cond_grad, (1, 0, 2)).reshape(local_latents, width)
    silu_pull = jax.vjp(silu_of, condition.astype(jnp.float32))[1]
    condition_grad = silu_pull(cond_grad)[0]

    waits = ([back],)
    attention_sum = jnp.concatenate([part.finish(*waits) for part in attention_sum], axis=0)
    expansion_sum = around(
        by_distance(expansion_sum.reshape(hidden_piece, seq_size, row_share), 1)
    )
    expansion_sum = jnp.concatenate(in_order(expansion_sum), axis=0).T
    contraction_sum = jnp.stack(in_order(around(contraction_sum)), axis=0).reshape(
        seq_size, proj_share, dp_size // seq_size, hidden_piece
    )
    contraction_sum = jnp.transpose(contraction_sum, (2, 0, 3, 1)).reshape(
        contraction_weight.shape
    )
    gradients = (
        modulation_sum,
        attention_sum[:qkv_share, :row_share].astype(jnp.float32).T,
        attention_sum[qkv_share:, :row_share].astype(jnp.float32).T,
        expansion_sum.astype(jnp.float32),
        contraction_sum.astype(jnp.float32),
    )

    step_rate = 0.06 / math.sqrt(all_latents * SEQ_LEN)
    masters = (
        modulation_weight,
        attention_weight,
        projection_weight,
        expansion_weight,
        contraction_weight,
    )
    moments = (
        modulation_moment,
        attention_moment,
        projection_moment,
        expansion_moment,
        contraction_moment,
    )
    averages = (
        modulation_average,
        attention_average,
        projection_average,
        expansion_average,
        contraction_average,
    )
    weight_next = []
    moment_next = []
    average_next = []
    for master, gradient, moment, average in zip(masters, gradients, moments, averages):
        moment_new = 0.5 * moment + gradient
        master_new = master - step_rate * (gradient + 0.5 * moment_new)
        weight_next.append(master_new)
        moment_next.append(moment_new)
        average_next.append(0.5 * average + 0.5 * master_new)
    return (
        block_output,
        masked_loss,
        latent_grad,
        condition_grad,
        *weight_next,
        *moment_next,
        *average_next,
    )


def solution(mesh):
    tokens_spec = P("dp", "seq", None)
    weight_spec = P("seq", "dp")
    in_specs = (
        tokens_spec,
        P("dp", None),
        tokens_spec,
        tokens_spec,
        P("dp", "seq"),
    ) + (weight_spec,) * 15
    out_specs = (tokens_spec, P(), tokens_spec, P("dp", None)) + (weight_spec,) * 15
    return jax.shard_map(body, mesh=mesh, in_specs=in_specs, out_specs=out_specs, check_vma=False)
```

```python
import math

import jax
import jax.numpy as jnp
from jax import lax
from jax.experimental import pallas as pl
from jax.experimental.pallas import tpu as pltpu
from jax.sharding import PartitionSpec as P

HEADS = 16
SEQ_LEN = 1024

epsilon = 1e-06
log2_e = math.log2(math.e)
low = jnp.bfloat16


def silu_of(values):
    return values * jax.nn.sigmoid(values)


def gelu_of(values):
    square = values * values
    tanh = jnp.tanh(values * (0.7978845608028654 + (0.044715 * 0.7978845608028654) * square))
    half = 0.5 * tanh + 0.5
    value = values * half
    inner = 2 * 0.7978845608028654 + (6 * 0.044715 * 0.7978845608028654) * square
    return value, half + (value - value * half) * inner


def modulated(values, offset, stretch):
    centered = values - jnp.mean(values, axis=-1, keepdims=True)
    variance = jnp.mean(centered * centered, axis=-1, keepdims=True)
    return centered * lax.rsqrt(variance + epsilon) * (1.0 + stretch) + offset


def dot(first, second, over):
    return lax.dot_general(first, second, (over, ((), ())), preferred_element_type=jnp.float32)


def nn(first, second):
    return dot(first, second, ((1,), (0,)))


def nt(first, second):
    return dot(first, second, ((1,), (1,)))


def tn(first, second):
    return dot(first, second, ((0,), (0,)))


def around(pieces):
    size = lax.axis_size("seq")
    got = [pieces[0]] * size
    for r in range(1, size):
        steps = [(j, (j + r) % size) for j in range(size)]
        got[(size - r) % size] = lax.ppermute(pieces[r], "seq", steps)
    return got


def in_order(got):
    size = lax.axis_size("seq")
    me = lax.axis_index("seq")
    if size == 2:
        return [jnp.where(me == 0, got[0], got[1]), jnp.where(me == 0, got[1], got[0])]
    stacked = jnp.stack(got)
    return [lax.dynamic_index_in_dim(stacked, (j - me) % size, 0, False) for j in range(size)]


def by_distance(array, axis):
    size = lax.axis_size("seq")
    me = lax.axis_index("seq")
    return [lax.dynamic_index_in_dim(array, (me + r) % size, axis, False) for r in range(size)]


def gather_tokens(own):
    return lax.optimization_barrier(
        jnp.concatenate(around([own] * lax.axis_size("seq")), axis=0)
    )


def sum_tokens(parts):
    got = around(parts[:1] + [lax.optimization_barrier(part) for part in parts[1:]])
    return sum([lax.optimization_barrier(got[0])] + got[1:])


def swap(array, bit):
    size = lax.axis_size("dp")
    return lax.ppermute(array, "dp", [(j, j ^ bit) for j in range(size)])


def hypercube():
    size = lax.axis_size("dp")
    return size >= 4 and size & (size - 1) == 0


nothing = pl.CostEstimate(flops=0, bytes_accessed=0, transcendentals=0)
in_hbm = pl.BlockSpec(memory_space=pltpu.HBM)


def after(value, *others):
    def kernel(*refs):
        pass

    if not others:
        return value
    return pl.pallas_call(
        kernel,
        out_shape=jax.ShapeDtypeStruct(value.shape, value.dtype),
        in_specs=[in_hbm] * (1 + len(others)),
        out_specs=in_hbm,
        input_output_aliases={0: 0},
        cost_estimate=nothing,
    )(value, *others)


def place(*ways):
    size = lax.axis_size("dp")
    count = len(ways)
    me = lax.axis_index("dp").astype(jnp.int32)
    index = (jnp.array([steps for _, steps in ways], jnp.int32) ^ me) & 3

    def kernel(index_ref, *refs):
        sources, targets = refs[: 4 * count], refs[4 * count : 5 * count]
        held, (arrived, left) = refs[5 * count : 6 * count], refs[6 * count :]
        inward, outward = [], []
        for n in range(4):
            for w in range(count):
                copy = pltpu.make_async_copy(sources[4 * w + n], held[w].at[n], arrived.at[w, n])
                copy.start()
                inward.append(copy)
        for n in range(4):
            for w in range(count):
                inward[n * count + w].wait()
                target = targets[w].at[:, index_ref[w, n]]
                copy = pltpu.make_async_copy(held[w].at[n], target, left.at[w, n])
                copy.start()
                outward.append(copy)
        for copy in outward:
            copy.wait()

    groups = [pieces[0].shape for pieces, _ in ways]
    placed = pl.pallas_call(
        kernel,
        out_shape=[jax.ShapeDtypeStruct((g[0], 4) + g[1:], low) for g in groups],
        in_specs=[pl.BlockSpec(memory_space=pltpu.SMEM)] + [in_hbm] * (4 * count),
        out_specs=[in_hbm] * count,
        scratch_shapes=[pltpu.VMEM((4,) + g, low) for g in groups]
        + [pltpu.SemaphoreType.DMA((count, 4))] * 2,
        compiler_params=pltpu.CompilerParams(vmem_limit_bytes=24 << 20),
        cost_estimate=nothing,
    )(index, *[piece for pieces, _ in ways for piece in pieces])
    return [whole.reshape((size,) + whole.shape[2:]) for whole in placed]


def gather_high(shard):
    if not hypercube():
        return shard
    held, bit = shard[None], lax.axis_size("dp") >> 1
    while bit >= 4:
        came = swap(held, bit)
        upper = (lax.axis_index("dp") & bit) != 0
        pair = [jnp.where(upper, came, held), jnp.where(upper, held, came)]
        held = jnp.stack(pair, axis=1).reshape((-1,) + held.shape[1:])
        bit >>= 1
    return held


class Low:
    def __init__(self, held, first, last):
        self.held, self.first, self.last = held, first, last
        if not hypercube():
            self.all = lax.all_gather(held, "dp", axis=0)
            return
        self.by_first = swap(held, first)
        self.by_last = swap(held, last)
        self.by_both = swap(self.by_first, last)

    def pieces(self):
        steps = (0, self.first, self.last, self.first | self.last)
        return [self.held, self.by_first, self.by_last, self.by_both], steps


def wholes(*ways):
    if not hypercube():
        return [way.all for way in ways]
    return place(*[way.pieces() for way in ways])


def plus(*parts):
    return sum(part.astype(jnp.float32) for part in parts).astype(parts[0].dtype)


class Sum:
    def __init__(self, blocks, first, last):
        self.blocks, self.first, self.last = blocks, first, last
        size = lax.axis_size("dp")
        if not hypercube():
            self.sent = []
            return
        me = lax.axis_index("dp")

        def group(distance):
            want = (me ^ distance) & 3
            parts = []
            for block in blocks:
                shape = block.shape[1:]
                part = lax.dynamic_slice(
                    block.reshape((size // 4, 2, 2) + shape),
                    (0, want >> 1, want & 1) + (0,) * len(shape),
                    (size // 4, 1, 1) + shape,
                )
                parts.append(part.reshape((size // 4,) + shape))
            return jnp.concatenate(parts, axis=1)

        self.sent = [group(first | last), group(first)]
        self.far = swap(self.sent[0], first)
        self.near = swap(self.sent[1], first)
        self.kept = group(last), group(0)

    def second(self, *others):
        self.passed = []
        if hypercube():
            self.onward = plus(self.kept[0], after(self.far, *others))
            self.passed = [self.onward]

    def third(self, *others):
        self.held = []
        if hypercube():
            through = swap(after(self.onward, *others), self.last)
            self.total = plus(self.kept[1], self.near, through)
            self.held = [self.total]

    def finish(self, *waits):
        if not hypercube():
            blocks = jnp.concatenate(self.blocks, axis=1)
            return lax.psum_scatter(blocks, "dp", scatter_dimension=0, tiled=False)
        waits = list(waits)

        def came(array):
            return after(array, *waits.pop(0)) if waits else array

        me = lax.axis_index("dp")
        held, bit = self.total, 4
        while bit < lax.axis_size("dp"):
            pairs = held.reshape((held.shape[0] // 2, 2) + held.shape[1:])
            mine = (me // bit) & 1
            away = lax.dynamic_index_in_dim(pairs, 1 - mine, 1, False)
            held = plus(lax.dynamic_index_in_dim(pairs, mine, 1, False), came(swap(away, bit)))
            bit <<= 1
        return held[0]


def by_low(blocks):
    if not hypercube():
        return blocks
    return jnp.swapaxes(blocks.reshape((-1, 4) + blocks.shape[1:]), 0, 1)


def sum_low(blocks):
    if not hypercube():
        return blocks
    size = lax.axis_size("dp")
    groups = [[n + m for m in range(4)] for n in range(0, size, 4)]
    return lax.psum_scatter(blocks, "dp", axis_index_groups=groups, tiled=False)


def sum_high(blocks):
    if not hypercube():
        return lax.psum_scatter(blocks, "dp", tiled=False)
    size = lax.axis_size("dp")
    groups = [list(range(m, size, 4)) for m in range(4)]
    return lax.psum_scatter(blocks, "dp", axis_index_groups=groups, tiled=False)


def gather_small(own, *others):
    size = lax.axis_size("dp")
    if not hypercube():
        return lax.all_gather(own, "dp", axis=0)
    me = lax.axis_index("dp")
    held, bit = own[None], 1
    while bit < size:
        came = swap(held, bit)
        upper = (me & bit) != 0
        held = jnp.concatenate(
            [jnp.where(upper, came, held), jnp.where(upper, held, came)], axis=0
        )
        bit <<= 1
        if bit == 4:
            held = after(held, *others)
    return held


def sum_small(blocks):
    return jnp.sum(lax.all_to_all(blocks, "dp", 0, 0, tiled=True), axis=0)


def softmax_kernel(heads, head_size, block, qkv_ref, out_ref, low_ref, log_ref, key_ref, value_ref):
    width, length = heads * head_size, qkv_ref.shape[1]
    for h in range(heads):
        cols = slice(h * head_size, (h + 1) * head_size)
        key_ref[...] = qkv_ref[0, :, width + h * head_size : width + (h + 1) * head_size]
        value_ref[...] = qkv_ref[0, :, 2 * width + h * head_size : 2 * width + (h + 1) * head_size]
        for b in range(length // block):
            rows = slice(b * block, (b + 1) * block)
            scores = nt(qkv_ref[0, rows, cols], key_ref[...]) * (head_size ** (-0.5) * log2_e)
            top = jnp.max(scores, axis=1, keepdims=True)
            raised = jnp.exp2(scores - top)
            total = jnp.sum(raised, axis=1, keepdims=True)
            out = nn(raised.astype(low), value_ref[...]) / total
            out_ref[0, rows, cols] = out
            low_ref[0, rows, cols] = out.astype(low)
            log_ref[0, h : h + 1, rows] = (top + jnp.log2(total)).T


def one_latent(*shape):
    return pl.BlockSpec((1,) + shape, lambda i: (i, 0, 0))


def attend(qkv, heads, head_size):
    latents, length, columns = qkv.shape
    width = heads * head_size
    return pl.pallas_call(
        lambda *refs: softmax_kernel(heads, head_size, math.gcd(length, 256), *refs),
        out_shape=(
            jax.ShapeDtypeStruct((latents, length, width), jnp.float32),
            jax.ShapeDtypeStruct((latents, length, width), low),
            jax.ShapeDtypeStruct((latents, heads, length), jnp.float32),
        ),
        grid=(latents,),
        in_specs=[one_latent(length, columns)],
        out_specs=(
            one_latent(length, width),
            one_latent(length, width),
            one_latent(heads, length),
        ),
        scratch_shapes=[pltpu.VMEM((length, head_size), low)] * 2,
        compiler_params=pltpu.CompilerParams(vmem_limit_bytes=48 << 20),
        cost_estimate=pl.CostEstimate(
            flops=4 * latents * length * length * width,
            bytes_accessed=10 * latents * heads * length * length,
            transcendentals=latents * heads * length * length,
        ),
    )(qkv)


def softmax_back_kernel(
    heads,
    head_size,
    block,
    qkv_ref,
    grad_ref,
    out_ref,
    log_ref,
    qkv_grad_ref,
    key_ref,
    value_ref,
    key_sum,
    value_sum,
):
    width, length = heads * head_size, qkv_ref.shape[1]
    scale = head_size ** (-0.5)
    for h in range(heads):
        cols = slice(h * head_size, (h + 1) * head_size)
        key_cols = slice(width + h * head_size, width + (h + 1) * head_size)
        value_cols = slice(2 * width + h * head_size, 2 * width + (h + 1) * head_size)
        key_ref[...] = qkv_ref[0, :, key_cols]
        value_ref[...] = qkv_ref[0, :, value_cols]
        for b in range(length // block):
            rows = slice(b * block, (b + 1) * block)
            query, grad = qkv_ref[0, rows, cols], grad_ref[0, rows, cols]
            delta = jnp.sum(
                (grad.astype(jnp.float32) * out_ref[0, rows, cols]).T, axis=0, keepdims=True
            )
            probability = jnp.exp2(
                nt(key_ref[...], query) * (scale * log2_e) - log_ref[0, h : h + 1, rows]
            )
            score_grad = (probability * (nt(value_ref[...], grad) - delta)).astype(low)
            key_part = nn(score_grad, query)
            value_part = nn(probability.astype(low), grad)
            key_sum[...] = key_part if b == 0 else key_sum[...] + key_part
            value_sum[...] = value_part if b == 0 else value_sum[...] + value_part
            qkv_grad_ref[0, rows, cols] = (tn(score_grad, key_ref[...]) * scale).astype(low)
        qkv_grad_ref[0, :, key_cols] = (key_sum[...] * scale).astype(low)
        qkv_grad_ref[0, :, value_cols] = value_sum[...].astype(low)


def attend_back(qkv, grad, out, log_total, heads, head_size):
    latents, length, columns = qkv.shape
    width = heads * head_size
    return pl.pallas_call(
        lambda *refs: softmax_back_kernel(heads, head_size, math.gcd(length, 512), *refs),
        out_shape=jax.ShapeDtypeStruct((latents, length, columns), low),
        grid=(latents,),
        in_specs=[
            one_latent(length, columns),
            one_latent(length, width),
            one_latent(length, width),
            one_latent(heads, length),
        ],
        out_specs=one_latent(length, columns),
        scratch_shapes=[pltpu.VMEM((length, head_size), low)] * 2
        + [pltpu.VMEM((length, head_size), jnp.float32)] * 2,
        compiler_params=pltpu.CompilerParams(vmem_limit_bytes=56 << 20),
        cost_estimate=nothing,
    )(qkv, grad, out, log_total)


def body(
    latents,
    condition,
    cotangent,
    teacher,
    valid_mask,
    modulation_weight,
    attention_weight,
    projection_weight,
    expansion_weight,
    contraction_weight,
    modulation_moment,
    attention_moment,
    projection_moment,
    expansion_moment,
    contraction_moment,
    modulation_average,
    attention_average,
    projection_average,
    expansion_average,
    contraction_average,
):
    local_latents, block_rows, width = latents.shape
    seq_size, dp_size = lax.axis_size("seq"), lax.axis_size("dp")
    seq_me, dp_me = lax.axis_index("seq"), lax.axis_index("dp")
    all_latents = local_latents * dp_size
    head_size = width // HEADS
    heads = HEADS // seq_size
    own_width = heads * head_size
    score_scale = head_size ** (-0.5)
    own_tokens = local_latents * block_rows
    tokens = own_tokens * seq_size
    row_share = attention_weight.shape[0]
    mod_share = modulation_weight.shape[1]
    qkv_share = attention_weight.shape[1]
    proj_share = projection_weight.shape[1]
    hidden_share = expansion_weight.shape[1]
    hidden_piece = hidden_share // seq_size

    row_room = (row_share + 127) // 128 * 128

    def roomy(array):
        return jnp.pad(array, [(0, 0)] * (array.ndim - 1) + [(0, row_room - array.shape[-1])])

    attention_low = roomy(attention_weight.astype(low).T)
    expansion_low = after(expansion_weight.astype(low).T, attention_low)
    expansion_low = expansion_low.reshape(seq_size, hidden_piece, row_share)
    expansion_shard = jnp.concatenate(in_order(around(by_distance(expansion_low, 0))), axis=1)
    contraction_low = after(contraction_weight.astype(low), attention_low).reshape(
        dp_size // seq_size, seq_size, hidden_piece, proj_share
    )
    contraction_shard = jnp.concatenate(in_order(around(by_distance(contraction_low, 1))), axis=0)
    contraction_shard = contraction_shard.reshape(dp_size * hidden_piece, proj_share).T
    projection_low = projection_weight.astype(low).T

    def widen(shard):
        rows, columns = shard.shape
        if columns >= width:
            return jnp.concatenate(jnp.split(shard, columns // width, axis=1), axis=0)
        return jnp.concatenate(jnp.split(shard, width // columns, axis=0), axis=1)

    def narrow(wide, rows):
        if wide.shape[-2] >= rows:
            return jnp.concatenate(jnp.split(wide, wide.shape[-2] // rows, axis=-2), axis=-1)
        return jnp.concatenate(jnp.split(wide, rows // wide.shape[-2], axis=-1), axis=-2)

    def widen_blocks(blocks):
        return jax.vmap(widen)(blocks)

    rides = width % own_width == 0 and proj_share % (width // own_width) == 0
    one = [widen(contraction_shard), expansion_shard]
    if rides:
        one.append(widen(projection_low))
    cut_c = one[0].shape[0]
    cut_e = cut_c + hidden_piece
    one_full = lax.all_gather(jnp.concatenate(one, axis=0), "dp", axis=0)
    if not rides:
        projection_full = lax.all_gather(projection_low, "dp", axis=0)

    attention_high = gather_high(attention_low)
    first_ready = [attention_high]
    half = (qkv_share // 2 + 15) // 16 * 16
    attention_a = Low(attention_high[..., :half, :], 1, 2)
    attention_b = Low(attention_high[..., half:, :], 2, 1)

    mask_float = valid_mask.astype(jnp.float32)
    chunk = math.gcd(own_tokens, 128)
    counts = jnp.sum(mask_float.reshape(own_tokens // chunk, chunk), axis=1).astype(low)
    packed = jnp.concatenate([condition.reshape(-1), counts])
    packed = gather_small(jnp.stack(in_order(around([packed] * seq_size))), *first_ready)
    count_total = jnp.sum(packed[:, :, local_latents * width :].astype(jnp.float32))
    every_cond = packed[:, 0, : local_latents * width].reshape(all_latents, width)
    cond_active = silu_of(every_cond.astype(jnp.float32)).astype(low)
    cond_rows = lax.dynamic_slice(
        cond_active, (0, seq_me * row_share), (all_latents, row_share)
    )
    attention_rows = jnp.concatenate(wholes(attention_a, attention_b), axis=1)
    attention_rows = attention_rows.reshape(3, seq_size, own_width, row_room)
    attention_full = jnp.concatenate(
        in_order(around(by_distance(attention_rows, 1))), axis=-1
    ).reshape(3 * own_width, seq_size * row_room)

    modulation_low = modulation_weight.astype(low)
    mod_part = nn(cond_rows, modulation_low).reshape(dp_size, local_latents, mod_share)
    mod_part = lax.all_to_all(mod_part, "dp", 0, 0, tiled=True)
    modulation = sum(around([mod_part] * seq_size))
    modulation = jnp.transpose(modulation, (1, 0, 2)).reshape(local_latents, dp_size * mod_share)
    shift_attn, scale_attn, gate_attn, shift_mlp, scale_mlp, gate_mlp = [
        group[:, None, :] for group in jnp.split(modulation, 6, axis=-1)
    ]

    residual_in = latents.astype(jnp.float32)
    attn_value, attn_pull = jax.vjp(modulated, residual_in, shift_attn, scale_attn)
    attn_input = roomy(attn_value.astype(low).reshape(own_tokens, seq_size, row_share))
    attn_input = gather_tokens(attn_input.reshape(own_tokens, seq_size * row_room))
    qkv_low = nt(attn_input, attention_full).astype(low)

    def by_latent(array):
        array = array.reshape(seq_size, local_latents, block_rows, -1)
        return jnp.transpose(array, (1, 0, 2, 3)).reshape(
            local_latents, seq_size * block_rows, -1
        )

    def by_device(array):
        array = array.reshape(local_latents, seq_size, block_rows, -1)
        return jnp.transpose(array, (1, 0, 2, 3)).reshape(tokens, -1)

    qkv = by_latent(qkv_low)
    attn_out, attn_low, log_total = attend(qkv, heads, head_size)
    attn_low = by_device(attn_low)

    one_full = after(one_full, attn_low)
    contraction_full = narrow(one_full[:, :cut_c], proj_share).reshape(
        width, dp_size * hidden_piece
    )
    expansion_full = one_full[:, cut_c:cut_e].reshape(dp_size * hidden_piece, width)
    if rides:
        projection_full = narrow(one_full[:, cut_e:], proj_share)
    projection_full = projection_full.reshape(width, own_width)

    def by_block(array):
        return [array[r * own_tokens : (r + 1) * own_tokens] for r in range(seq_size)]

    def own_shape(array):
        return array.reshape(local_latents, block_rows, width)

    proj_out = own_shape(sum_tokens([nt(rows, projection_full) for rows in by_block(attn_low)]))
    mid_resid = residual_in + gate_attn * proj_out

    mlp_value, mlp_pull = jax.vjp(modulated, mid_resid, shift_mlp, scale_mlp)
    mlp_input = gather_tokens(mlp_value.astype(low).reshape(own_tokens, width))
    value, slope = gelu_of(nt(mlp_input, expansion_full))
    hidden_low, hidden_slope = lax.optimization_barrier((value.astype(low), slope.astype(low)))
    mlp_out = own_shape(sum_tokens([nt(rows, contraction_full) for rows in by_block(hidden_low)]))
    block_output = mid_resid + gate_mlp * mlp_out

    teacher_gap = block_output - teacher.astype(jnp.float32)
    local_square = jnp.sum(mask_float[..., None] * teacher_gap * teacher_gap)
    out_grad = cotangent.astype(jnp.float32) + 2.0 * mask_float[..., None] * teacher_gap / (
        count_total * width
    )

    gate_mlp_grad = jnp.sum(out_grad * mlp_out, axis=1)
    mlp_out_grad = gather_tokens((gate_mlp * out_grad).astype(low).reshape(own_tokens, width))
    folds = max(dp_size * hidden_piece // width, 1)
    contraction_grad = [
        tn(mlp_out_grad, part).astype(low).reshape(dp_size, proj_share, -1)
        for part in jnp.split(hidden_low, folds, axis=1)
    ]
    hidden_grad = nn(mlp_out_grad, contraction_full)
    hidden_pre_grad = (hidden_grad * hidden_slope.astype(jnp.float32)).astype(low)
    expansion_grad = tn(hidden_pre_grad, mlp_input).astype(low)
    expansion_grad = expansion_grad.reshape(dp_size, hidden_piece, width)
    if contraction_grad[0].shape[-1] != width:
        contraction_grad = [widen_blocks(part) for part in contraction_grad]
    mlp_grads = by_low(jnp.concatenate(contraction_grad + [expansion_grad], axis=1))
    expansion_back = after(expansion_full, mlp_grads)
    mlp_sum = sum_low(mlp_grads)
    mlp_input_grad = own_shape(
        sum_tokens([nn(rows, expansion_back) for rows in by_block(hidden_pre_grad)])
    )
    mid_part, shift_mlp_grad, scale_mlp_grad = mlp_pull(mlp_input_grad)
    mid_grad = out_grad + mid_part

    gate_attn_grad = jnp.sum(mid_grad * proj_out, axis=1)
    proj_out_grad = gather_tokens((gate_attn * mid_grad).astype(low).reshape(own_tokens, width))
    projection_grad = tn(proj_out_grad, roomy(attn_low)).astype(low)
    attn_out_grad = by_latent(nn(proj_out_grad, projection_full).astype(low))
    qkv_grad = by_device(
        attend_back(qkv, attn_out_grad, attn_out, log_total, heads, head_size)
    )
    features = attn_input.reshape(tokens, seq_size, row_room)
    attention_grad = [
        tn(qkv_grad, columns).astype(low).reshape(3, own_width, row_room)
        for columns in by_distance(features, 1)
    ]
    attention_grad = jnp.stack(in_order(around(attention_grad)), axis=1).reshape(
        dp_size, qkv_share, row_room
    )
    projection_grad = projection_grad.reshape(dp_size, proj_share, row_room)
    sum_half = (qkv_share + proj_share) // 2
    attention_sum = [
        Sum([attention_grad[:, :sum_half]], 1, 2),
        Sum([attention_grad[:, sum_half:], projection_grad], 2, 1),
    ]
    qkv_grad = after(qkv_grad, *attention_sum[0].sent, *attention_sum[1].sent)
    attn_input_grad = sum_tokens([nn(rows, attention_full) for rows in by_block(qkv_grad)])
    attn_input_grad = attn_input_grad.reshape(own_tokens, seq_size, row_room)[..., :row_share]
    attn_input_grad = own_shape(attn_input_grad)
    resid_part, shift_attn_grad, scale_attn_grad = attn_pull(attn_input_grad)
    latent_grad = mid_grad + resid_part

    mod_grad = jnp.concatenate(
        [
            shift_attn_grad[:, 0, :],
            scale_attn_grad[:, 0, :],
            gate_attn_grad,
            shift_mlp_grad[:, 0, :],
            scale_mlp_grad[:, 0, :],
            gate_mlp_grad,
        ],
        axis=-1,
    )
    mod_local = mod_grad
    mod_grad = sum(around([mod_grad] * seq_size)).astype(low)
    mod_grad = jnp.transpose(mod_grad.reshape(local_latents, dp_size, mod_share), (1, 0, 2))
    mod_grad = lax.all_to_all(mod_grad, "dp", 0, 0, tiled=True).reshape(all_latents, mod_share)
    for part in attention_sum:
        part.second(mod_local)
    for part in attention_sum:
        part.third(mod_grad)
    modulation_sum = tn(cond_rows, mod_grad)
    cond_part = nt(mod_grad, modulation_low).reshape(dp_size, local_latents * row_share)
    squares = jnp.broadcast_to(local_square, (dp_size, 128))
    back = sum_small(jnp.concatenate([cond_part, squares], axis=1))[None]
    back = after(back, *attention_sum[0].held, *attention_sum[1].held)
    back = jnp.stack(in_order(around([back] * seq_size)), axis=0)
    square_total = jnp.sum(back[:, 0, local_latents * row_share])
    masked_loss = square_total / (count_total * width)
    cond_grad = back[:, 0, : local_latents * row_share].reshape(seq_size, local_latents, row_share)
    cond_grad = jnp.transpose(cond_grad, (1, 0, 2)).reshape(local_latents, width)
    silu_pull = jax.vjp(silu_of, condition.astype(jnp.float32))[1]
    condition_grad = silu_pull(cond_grad)[0]

    mlp_sum = sum_high(after(mlp_sum, mod_grad))
    if cut_c == seq_size * proj_share:
        contraction_sum = by_distance(mlp_sum[:cut_c].reshape(seq_size, proj_share, width), 0)
    else:
        contraction_sum = narrow(mlp_sum[:cut_c], proj_share).reshape(proj_share, seq_size, -1)
        contraction_sum = by_distance(contraction_sum, 1)
    expansion_sum = mlp_sum[cut_c:]
    waits = ([back],)
    attention_sum = jnp.concatenate([part.finish(*waits) for part in attention_sum], axis=0)
    expansion_sum = around(
        by_distance(expansion_sum.reshape(hidden_piece, seq_size, row_share), 1)
    )
    expansion_sum = jnp.concatenate(in_order(expansion_sum), axis=0).T
    contraction_sum = jnp.stack(in_order(around(contraction_sum)), axis=0).reshape(
        seq_size, proj_share, dp_size // seq_size, hidden_piece
    )
    contraction_sum = jnp.transpose(contraction_sum, (2, 0, 3, 1)).reshape(
        contraction_weight.shape
    )
    gradients = (
        modulation_sum,
        attention_sum[:qkv_share, :row_share].astype(jnp.float32).T,
        attention_sum[qkv_share:, :row_share].astype(jnp.float32).T,
        expansion_sum.astype(jnp.float32),
        contraction_sum.astype(jnp.float32),
    )

    step_rate = 0.06 / math.sqrt(all_latents * SEQ_LEN)
    masters = (
        modulation_weight,
        attention_weight,
        projection_weight,
        expansion_weight,
        contraction_weight,
    )
    moments = (
        modulation_moment,
        attention_moment,
        projection_moment,
        expansion_moment,
        contraction_moment,
    )
    averages = (
        modulation_average,
        attention_average,
        projection_average,
        expansion_average,
        contraction_average,
    )
    weight_next = []
    moment_next = []
    average_next = []
    for master, gradient, moment, average in zip(masters, gradients, moments, averages):
        moment_new = 0.5 * moment + gradient
        master_new = master - step_rate * (gradient + 0.5 * moment_new)
        weight_next.append(master_new)
        moment_next.append(moment_new)
        average_next.append(0.5 * average + 0.5 * master_new)
    return (
        block_output,
        masked_loss,
        latent_grad,
        condition_grad,
        *weight_next,
        *moment_next,
        *average_next,
    )


def solution(mesh):
    tokens_spec = P("dp", "seq", None)
    weight_spec = P("seq", "dp")
    in_specs = (
        tokens_spec,
        P("dp", None),
        tokens_spec,
        tokens_spec,
        P("dp", "seq"),
    ) + (weight_spec,) * 15
    out_specs = (tokens_spec, P(), tokens_spec, P("dp", None)) + (weight_spec,) * 15
    return jax.shard_map(body, mesh=mesh, in_specs=in_specs, out_specs=out_specs, check_vma=False)
```

```python
import math

import jax
import jax.numpy as jnp
from jax import lax
from jax.experimental import pallas as pl
from jax.experimental.pallas import tpu as pltpu
from jax.sharding import PartitionSpec as P

HEADS = 16
SEQ_LEN = 1024

epsilon = 1e-06
log2_e = math.log2(math.e)
low = jnp.bfloat16


def silu_of(values):
    return values * jax.nn.sigmoid(values)


def gelu_of(values):
    square = values * values
    tanh = jnp.tanh(values * (0.7978845608028654 + (0.044715 * 0.7978845608028654) * square))
    half = 0.5 * tanh + 0.5
    value = values * half
    inner = 2 * 0.7978845608028654 + (6 * 0.044715 * 0.7978845608028654) * square
    return value, half + (value - value * half) * inner


def modulated(values, offset, stretch):
    centered = values - jnp.mean(values, axis=-1, keepdims=True)
    variance = jnp.mean(centered * centered, axis=-1, keepdims=True)
    return centered * lax.rsqrt(variance + epsilon) * (1.0 + stretch) + offset


def dot(first, second, over):
    return lax.dot_general(first, second, (over, ((), ())), preferred_element_type=jnp.float32)


def nn(first, second):
    return dot(first, second, ((1,), (0,)))


def nt(first, second):
    return dot(first, second, ((1,), (1,)))


def tn(first, second):
    return dot(first, second, ((0,), (0,)))


def around(pieces):
    size = lax.axis_size("seq")
    got = [pieces[0]] * size
    for r in range(1, size):
        steps = [(j, (j + r) % size) for j in range(size)]
        got[(size - r) % size] = lax.ppermute(pieces[r], "seq", steps)
    return got


def in_order(got):
    size = lax.axis_size("seq")
    me = lax.axis_index("seq")
    if size == 2:
        return [jnp.where(me == 0, got[0], got[1]), jnp.where(me == 0, got[1], got[0])]
    stacked = jnp.stack(got)
    return [lax.dynamic_index_in_dim(stacked, (j - me) % size, 0, False) for j in range(size)]


def by_distance(array, axis):
    size = lax.axis_size("seq")
    me = lax.axis_index("seq")
    return [lax.dynamic_index_in_dim(array, (me + r) % size, axis, False) for r in range(size)]


def gather_tokens(own):
    return lax.optimization_barrier(
        jnp.concatenate(around([own] * lax.axis_size("seq")), axis=0)
    )


def sum_tokens(parts):
    got = around(parts[:1] + [lax.optimization_barrier(part) for part in parts[1:]])
    return sum([lax.optimization_barrier(got[0])] + got[1:])


def swap(array, bit):
    size = lax.axis_size("dp")
    return lax.ppermute(array, "dp", [(j, j ^ bit) for j in range(size)])


def hypercube():
    size = lax.axis_size("dp")
    return size >= 4 and size & (size - 1) == 0


nothing = pl.CostEstimate(flops=0, bytes_accessed=0, transcendentals=0)
in_hbm = pl.BlockSpec(memory_space=pltpu.HBM)


def after(value, *others):
    def kernel(*refs):
        pass

    if not others:
        return value
    return pl.pallas_call(
        kernel,
        out_shape=jax.ShapeDtypeStruct(value.shape, value.dtype),
        in_specs=[in_hbm] * (1 + len(others)),
        out_specs=in_hbm,
        input_output_aliases={0: 0},
        cost_estimate=nothing,
    )(value, *others)


def place(*ways):
    size = lax.axis_size("dp")
    count = len(ways)
    me = lax.axis_index("dp").astype(jnp.int32)
    index = (jnp.array([steps for _, steps in ways], jnp.int32) ^ me) & 3

    def kernel(index_ref, *refs):
        sources, targets = refs[: 4 * count], refs[4 * count : 5 * count]
        held, (arrived, left) = refs[5 * count : 6 * count], refs[6 * count :]
        inward, outward = [], []
        for n in range(4):
            for w in range(count):
                copy = pltpu.make_async_copy(sources[4 * w + n], held[w].at[n], arrived.at[w, n])
                copy.start()
                inward.append(copy)
        for n in range(4):
            for w in range(count):
                inward[n * count + w].wait()
                target = targets[w].at[:, index_ref[w, n]]
                copy = pltpu.make_async_copy(held[w].at[n], target, left.at[w, n])
                copy.start()
                outward.append(copy)
        for copy in outward:
            copy.wait()

    groups = [pieces[0].shape for pieces, _ in ways]
    placed = pl.pallas_call(
        kernel,
        out_shape=[jax.ShapeDtypeStruct((g[0], 4) + g[1:], low) for g in groups],
        in_specs=[pl.BlockSpec(memory_space=pltpu.SMEM)] + [in_hbm] * (4 * count),
        out_specs=[in_hbm] * count,
        scratch_shapes=[pltpu.VMEM((4,) + g, low) for g in groups]
        + [pltpu.SemaphoreType.DMA((count, 4))] * 2,
        compiler_params=pltpu.CompilerParams(vmem_limit_bytes=24 << 20),
        cost_estimate=nothing,
    )(index, *[piece for pieces, _ in ways for piece in pieces])
    return [whole.reshape((size,) + whole.shape[2:]) for whole in placed]


def gather_high(shard):
    if not hypercube():
        return shard
    held, bit = shard[None], lax.axis_size("dp") >> 1
    while bit >= 4:
        came = swap(held, bit)
        upper = (lax.axis_index("dp") & bit) != 0
        pair = [jnp.where(upper, came, held), jnp.where(upper, held, came)]
        held = jnp.stack(pair, axis=1).reshape((-1,) + held.shape[1:])
        bit >>= 1
    return held


class Low:
    def __init__(self, held, first, last):
        self.held, self.first, self.last = held, first, last
        if not hypercube():
            self.all = lax.all_gather(held, "dp", axis=0)
            return
        self.by_first = swap(held, first)
        self.by_last = swap(held, last)
        self.by_both = swap(self.by_first, last)

    def pieces(self):
        steps = (0, self.first, self.last, self.first | self.last)
        return [self.held, self.by_first, self.by_last, self.by_both], steps


def wholes(*ways):
    if not hypercube():
        return [way.all for way in ways]
    return place(*[way.pieces() for way in ways])


def plus(*parts):
    return sum(part.astype(jnp.float32) for part in parts).astype(parts[0].dtype)


class Sum:
    def __init__(self, blocks, first, last):
        self.blocks, self.first, self.last = blocks, first, last
        size = lax.axis_size("dp")
        if not hypercube():
            self.sent = []
            return
        me = lax.axis_index("dp")

        def group(distance):
            want = (me ^ distance) & 3
            parts = []
            for block in blocks:
                shape = block.shape[1:]
                part = lax.dynamic_slice(
                    block.reshape((size // 4, 2, 2) + shape),
                    (0, want >> 1, want & 1) + (0,) * len(shape),
                    (size // 4, 1, 1) + shape,
                )
                parts.append(part.reshape((size // 4,) + shape))
            return jnp.concatenate(parts, axis=1)

        self.sent = [group(first | last), group(first)]
        self.far = swap(self.sent[0], first)
        self.near = swap(self.sent[1], first)
        self.kept = group(last), group(0)

    def second(self, *others):
        self.passed = []
        if hypercube():
            self.onward = plus(self.kept[0], after(self.far, *others))
            self.passed = [self.onward]

    def third(self, *others):
        self.held = []
        if hypercube():
            through = swap(after(self.onward, *others), self.last)
            self.total = plus(self.kept[1], self.near, through)
            self.held = [self.total]

    def finish(self, *waits):
        if not hypercube():
            blocks = jnp.concatenate(self.blocks, axis=1)
            return lax.psum_scatter(blocks, "dp", scatter_dimension=0, tiled=False)
        waits = list(waits)

        def came(array):
            return after(array, *waits.pop(0)) if waits else array

        me = lax.axis_index("dp")
        held, bit = self.total, 4
        while bit < lax.axis_size("dp"):
            pairs = held.reshape((held.shape[0] // 2, 2) + held.shape[1:])
            mine = (me // bit) & 1
            away = lax.dynamic_index_in_dim(pairs, 1 - mine, 1, False)
            held = plus(lax.dynamic_index_in_dim(pairs, mine, 1, False), came(swap(away, bit)))
            bit <<= 1
        return held[0]


def by_low(blocks):
    if not hypercube():
        return blocks
    return jnp.swapaxes(blocks.reshape((-1, 4) + blocks.shape[1:]), 0, 1)


def sum_low(blocks):
    if not hypercube():
        return blocks
    size = lax.axis_size("dp")
    groups = [[n + m for m in range(4)] for n in range(0, size, 4)]
    return lax.psum_scatter(blocks, "dp", axis_index_groups=groups, tiled=False)


def sum_high(blocks):
    if not hypercube():
        return lax.psum_scatter(blocks, "dp", tiled=False)
    size = lax.axis_size("dp")
    groups = [list(range(m, size, 4)) for m in range(4)]
    return lax.psum_scatter(blocks, "dp", axis_index_groups=groups, tiled=False)


def gather_small(own, *others):
    size = lax.axis_size("dp")
    if not hypercube():
        return lax.all_gather(own, "dp", axis=0)
    me = lax.axis_index("dp")
    held, bit = own[None], 1
    while bit < size:
        came = swap(held, bit)
        upper = (me & bit) != 0
        held = jnp.concatenate(
            [jnp.where(upper, came, held), jnp.where(upper, held, came)], axis=0
        )
        bit <<= 1
        if bit == 4:
            held = after(held, *others)
    return held


def sum_small(blocks):
    return jnp.sum(lax.all_to_all(blocks, "dp", 0, 0, tiled=True), axis=0)


def softmax_kernel(heads, head_size, block, qkv_ref, out_ref, low_ref, log_ref, key_ref, value_ref):
    width, length = heads * head_size, qkv_ref.shape[1]
    for h in range(heads):
        cols = slice(h * head_size, (h + 1) * head_size)
        key_ref[...] = qkv_ref[0, :, width + h * head_size : width + (h + 1) * head_size]
        value_ref[...] = qkv_ref[0, :, 2 * width + h * head_size : 2 * width + (h + 1) * head_size]
        for b in range(length // block):
            rows = slice(b * block, (b + 1) * block)
            scores = nt(qkv_ref[0, rows, cols], key_ref[...]) * (head_size ** (-0.5) * log2_e)
            top = jnp.max(scores, axis=1, keepdims=True)
            raised = jnp.exp2(scores - top)
            total = jnp.sum(raised, axis=1, keepdims=True)
            out = nn(raised.astype(low), value_ref[...]) / total
            out_ref[0, rows, cols] = out
            low_ref[0, rows, cols] = out.astype(low)
            log_ref[0, h : h + 1, rows] = (top + jnp.log2(total)).T


def one_latent(*shape):
    return pl.BlockSpec((1,) + shape, lambda i: (i, 0, 0))


def attend(qkv, heads, head_size):
    latents, length, columns = qkv.shape
    width = heads * head_size
    return pl.pallas_call(
        lambda *refs: softmax_kernel(heads, head_size, math.gcd(length, 256), *refs),
        out_shape=(
            jax.ShapeDtypeStruct((latents, length, width), jnp.float32),
            jax.ShapeDtypeStruct((latents, length, width), low),
            jax.ShapeDtypeStruct((latents, heads, length), jnp.float32),
        ),
        grid=(latents,),
        in_specs=[one_latent(length, columns)],
        out_specs=(
            one_latent(length, width),
            one_latent(length, width),
            one_latent(heads, length),
        ),
        scratch_shapes=[pltpu.VMEM((length, head_size), low)] * 2,
        compiler_params=pltpu.CompilerParams(vmem_limit_bytes=48 << 20),
        cost_estimate=pl.CostEstimate(
            flops=4 * latents * length * length * width,
            bytes_accessed=10 * latents * heads * length * length,
            transcendentals=latents * heads * length * length,
        ),
    )(qkv)


def softmax_back_kernel(
    heads,
    head_size,
    block,
    qkv_ref,
    grad_ref,
    out_ref,
    log_ref,
    qkv_grad_ref,
    key_ref,
    value_ref,
    key_sum,
    value_sum,
):
    width, length = heads * head_size, qkv_ref.shape[1]
    scale = head_size ** (-0.5)
    for h in range(heads):
        cols = slice(h * head_size, (h + 1) * head_size)
        key_cols = slice(width + h * head_size, width + (h + 1) * head_size)
        value_cols = slice(2 * width + h * head_size, 2 * width + (h + 1) * head_size)
        key_ref[...] = qkv_ref[0, :, key_cols]
        value_ref[...] = qkv_ref[0, :, value_cols]
        for b in range(length // block):
            rows = slice(b * block, (b + 1) * block)
            query, grad = qkv_ref[0, rows, cols], grad_ref[0, rows, cols]
            delta = jnp.sum(
                (grad.astype(jnp.float32) * out_ref[0, rows, cols]).T, axis=0, keepdims=True
            )
            probability = jnp.exp2(
                nt(key_ref[...], query) * (scale * log2_e) - log_ref[0, h : h + 1, rows]
            )
            score_grad = (probability * (nt(value_ref[...], grad) - delta)).astype(low)
            key_part = nn(score_grad, query)
            value_part = nn(probability.astype(low), grad)
            key_sum[...] = key_part if b == 0 else key_sum[...] + key_part
            value_sum[...] = value_part if b == 0 else value_sum[...] + value_part
            qkv_grad_ref[0, rows, cols] = (tn(score_grad, key_ref[...]) * scale).astype(low)
        qkv_grad_ref[0, :, key_cols] = (key_sum[...] * scale).astype(low)
        qkv_grad_ref[0, :, value_cols] = value_sum[...].astype(low)


def attend_back(qkv, grad, out, log_total, heads, head_size):
    latents, length, columns = qkv.shape
    width = heads * head_size
    return pl.pallas_call(
        lambda *refs: softmax_back_kernel(heads, head_size, math.gcd(length, 512), *refs),
        out_shape=jax.ShapeDtypeStruct((latents, length, columns), low),
        grid=(latents,),
        in_specs=[
            one_latent(length, columns),
            one_latent(length, width),
            one_latent(length, width),
            one_latent(heads, length),
        ],
        out_specs=one_latent(length, columns),
        scratch_shapes=[pltpu.VMEM((length, head_size), low)] * 2
        + [pltpu.VMEM((length, head_size), jnp.float32)] * 2,
        compiler_params=pltpu.CompilerParams(vmem_limit_bytes=56 << 20),
        cost_estimate=nothing,
    )(qkv, grad, out, log_total)


def body(
    latents,
    condition,
    cotangent,
    teacher,
    valid_mask,
    modulation_weight,
    attention_weight,
    projection_weight,
    expansion_weight,
    contraction_weight,
    modulation_moment,
    attention_moment,
    projection_moment,
    expansion_moment,
    contraction_moment,
    modulation_average,
    attention_average,
    projection_average,
    expansion_average,
    contraction_average,
):
    local_latents, block_rows, width = latents.shape
    seq_size, dp_size = lax.axis_size("seq"), lax.axis_size("dp")
    seq_me, dp_me = lax.axis_index("seq"), lax.axis_index("dp")
    all_latents = local_latents * dp_size
    head_size = width // HEADS
    heads = HEADS // seq_size
    own_width = heads * head_size
    score_scale = head_size ** (-0.5)
    own_tokens = local_latents * block_rows
    tokens = own_tokens * seq_size
    row_share = attention_weight.shape[0]
    mod_share = modulation_weight.shape[1]
    qkv_share = attention_weight.shape[1]
    proj_share = projection_weight.shape[1]
    hidden_share = expansion_weight.shape[1]
    hidden_piece = hidden_share // seq_size

    row_room = (row_share + 127) // 128 * 128

    def roomy(array):
        return jnp.pad(array, [(0, 0)] * (array.ndim - 1) + [(0, row_room - array.shape[-1])])

    attention_low = roomy(attention_weight.astype(low).T)
    expansion_low = after(expansion_weight.astype(low).T, attention_low)
    expansion_low = expansion_low.reshape(seq_size, hidden_piece, row_share)
    expansion_shard = jnp.concatenate(in_order(around(by_distance(expansion_low, 0))), axis=1)
    contraction_low = after(contraction_weight.astype(low), attention_low).reshape(
        dp_size // seq_size, seq_size, hidden_piece, proj_share
    )
    contraction_shard = jnp.concatenate(in_order(around(by_distance(contraction_low, 1))), axis=0)
    contraction_shard = contraction_shard.reshape(dp_size * hidden_piece, proj_share).T
    projection_low = projection_weight.astype(low).T

    def widen(shard):
        rows, columns = shard.shape
        if columns >= width:
            return jnp.concatenate(jnp.split(shard, columns // width, axis=1), axis=0)
        return jnp.concatenate(jnp.split(shard, width // columns, axis=0), axis=1)

    def narrow(wide, rows):
        if wide.shape[-2] >= rows:
            return jnp.concatenate(jnp.split(wide, wide.shape[-2] // rows, axis=-2), axis=-1)
        return jnp.concatenate(jnp.split(wide, rows // wide.shape[-2], axis=-1), axis=-2)

    def widen_blocks(blocks):
        return jax.vmap(widen)(blocks)

    rides = width % own_width == 0 and proj_share % (width // own_width) == 0
    one = [widen(contraction_shard), expansion_shard]
    if rides:
        one.append(widen(projection_low))
    cut_c = one[0].shape[0]
    cut_e = cut_c + hidden_piece
    one_full = lax.all_gather(jnp.concatenate(one, axis=0), "dp", axis=0)
    if not rides:
        projection_full = lax.all_gather(projection_low, "dp", axis=0)

    attention_high = gather_high(attention_low)
    first_ready = [attention_high]
    half = (qkv_share // 2 + 15) // 16 * 16
    attention_a = Low(attention_high[..., :half, :], 1, 2)
    attention_b = Low(attention_high[..., half:, :], 2, 1)

    mask_float = valid_mask.astype(jnp.float32)
    chunk = math.gcd(own_tokens, 128)
    counts = jnp.sum(mask_float.reshape(own_tokens // chunk, chunk), axis=1).astype(low)
    packed = jnp.concatenate([condition.reshape(-1), counts])
    packed = gather_small(jnp.stack(in_order(around([packed] * seq_size))), *first_ready)
    count_total = jnp.sum(packed[:, :, local_latents * width :].astype(jnp.float32))
    every_cond = packed[:, 0, : local_latents * width].reshape(all_latents, width)
    cond_active = silu_of(every_cond.astype(jnp.float32)).astype(low)
    cond_rows = lax.dynamic_slice(
        cond_active, (0, seq_me * row_share), (all_latents, row_share)
    )
    attention_rows = jnp.concatenate(wholes(attention_a, attention_b), axis=1)
    attention_rows = attention_rows.reshape(3, seq_size, own_width, row_room)
    attention_full = jnp.concatenate(
        in_order(around(by_distance(attention_rows, 1))), axis=-1
    ).reshape(3 * own_width, seq_size * row_room)

    modulation_low = modulation_weight.astype(low)
    mod_part = nn(cond_rows, modulation_low).reshape(dp_size, local_latents, mod_share)
    mod_part = lax.all_to_all(mod_part, "dp", 0, 0, tiled=True)
    modulation = sum(around([mod_part] * seq_size))
    modulation = jnp.transpose(modulation, (1, 0, 2)).reshape(local_latents, dp_size * mod_share)
    shift_attn, scale_attn, gate_attn, shift_mlp, scale_mlp, gate_mlp = [
        group[:, None, :] for group in jnp.split(modulation, 6, axis=-1)
    ]

    residual_in = latents.astype(jnp.float32)
    attn_value, attn_pull = jax.vjp(modulated, residual_in, shift_attn, scale_attn)
    attn_input = roomy(attn_value.astype(low).reshape(own_tokens, seq_size, row_share))
    attn_input = gather_tokens(attn_input.reshape(own_tokens, seq_size * row_room))
    qkv_low = nt(attn_input, attention_full).astype(low)

    def by_latent(array):
        array = array.reshape(seq_size, local_latents, block_rows, -1)
        return jnp.transpose(array, (1, 0, 2, 3)).reshape(
            local_latents, seq_size * block_rows, -1
        )

    def by_device(array):
        array = array.reshape(local_latents, seq_size, block_rows, -1)
        return jnp.transpose(array, (1, 0, 2, 3)).reshape(tokens, -1)

    qkv = by_latent(qkv_low)
    attn_out, attn_low, log_total = attend(qkv, heads, head_size)
    attn_low = by_device(attn_low)

    one_full = after(one_full, attn_low)
    contraction_full = narrow(one_full[:, :cut_c], proj_share).reshape(
        width, dp_size * hidden_piece
    )
    expansion_full = one_full[:, cut_c:cut_e].reshape(dp_size * hidden_piece, width)
    if rides:
        projection_full = narrow(one_full[:, cut_e:], proj_share)
    projection_full = projection_full.reshape(width, own_width)

    def by_block(array):
        return [array[r * own_tokens : (r + 1) * own_tokens] for r in range(seq_size)]

    def own_shape(array):
        return array.reshape(local_latents, block_rows, width)

    proj_out = own_shape(sum_tokens([nt(rows, projection_full) for rows in by_block(attn_low)]))
    mid_resid = residual_in + gate_attn * proj_out

    mlp_value, mlp_pull = jax.vjp(modulated, mid_resid, shift_mlp, scale_mlp)
    mlp_input = gather_tokens(mlp_value.astype(low).reshape(own_tokens, width))
    value, slope = gelu_of(nt(mlp_input, expansion_full))
    hidden_low, hidden_slope = lax.optimization_barrier((value.astype(low), slope.astype(low)))
    mlp_out = own_shape(sum_tokens([nt(rows, contraction_full) for rows in by_block(hidden_low)]))
    block_output = mid_resid + gate_mlp * mlp_out

    teacher_gap = block_output - teacher.astype(jnp.float32)
    local_square = jnp.sum(mask_float[..., None] * teacher_gap * teacher_gap)
    out_grad = cotangent.astype(jnp.float32) + 2.0 * mask_float[..., None] * teacher_gap / (
        count_total * width
    )

    gate_mlp_grad = jnp.sum(out_grad * mlp_out, axis=1)
    mlp_out_grad = gather_tokens((gate_mlp * out_grad).astype(low).reshape(own_tokens, width))
    folds = max(dp_size * hidden_piece // width, 1)
    contraction_grad = [
        tn(mlp_out_grad, part).astype(low).reshape(dp_size, proj_share, -1)
        for part in jnp.split(hidden_low, folds, axis=1)
    ]
    hidden_grad = nn(mlp_out_grad, contraction_full)
    hidden_pre_grad = (hidden_grad * hidden_slope.astype(jnp.float32)).astype(low)
    expansion_grad = tn(hidden_pre_grad, mlp_input).astype(low)
    expansion_grad = expansion_grad.reshape(dp_size, hidden_piece, width)
    if contraction_grad[0].shape[-1] != width:
        contraction_grad = [widen_blocks(part) for part in contraction_grad]
    mlp_grads = by_low(jnp.concatenate(contraction_grad + [expansion_grad], axis=1))
    expansion_back = after(expansion_full, mlp_grads)
    mlp_sum = sum_low(mlp_grads)
    mlp_input_grad = own_shape(
        sum_tokens([nn(rows, expansion_back) for rows in by_block(hidden_pre_grad)])
    )
    mid_part, shift_mlp_grad, scale_mlp_grad = mlp_pull(mlp_input_grad)
    mid_grad = out_grad + mid_part

    gate_attn_grad = jnp.sum(mid_grad * proj_out, axis=1)
    proj_out_grad = gather_tokens((gate_attn * mid_grad).astype(low).reshape(own_tokens, width))
    projection_grad = tn(proj_out_grad, roomy(attn_low)).astype(low)
    attn_out_grad = by_latent(nn(proj_out_grad, projection_full).astype(low))
    qkv_grad = by_device(
        attend_back(qkv, attn_out_grad, attn_out, log_total, heads, head_size)
    )
    features = attn_input.reshape(tokens, seq_size, row_room)
    attention_grad = [
        tn(qkv_grad, columns).astype(low).reshape(3, own_width, row_room)
        for columns in by_distance(features, 1)
    ]
    attention_grad = jnp.stack(in_order(around(attention_grad)), axis=1).reshape(
        dp_size, qkv_share, row_room
    )
    projection_grad = projection_grad.reshape(dp_size, proj_share, row_room)
    sum_half = (qkv_share + proj_share) // 2
    attention_sum = [
        Sum([attention_grad[:, :sum_half]], 1, 2),
        Sum([attention_grad[:, sum_half:], projection_grad], 2, 1),
    ]
    qkv_grad = after(qkv_grad, *attention_sum[0].sent, *attention_sum[1].sent)
    attn_input_grad = sum_tokens([nn(rows, attention_full) for rows in by_block(qkv_grad)])
    attn_input_grad = attn_input_grad.reshape(own_tokens, seq_size, row_room)[..., :row_share]
    attn_input_grad = own_shape(attn_input_grad)
    resid_part, shift_attn_grad, scale_attn_grad = attn_pull(attn_input_grad)
    latent_grad = mid_grad + resid_part

    mod_grad = jnp.concatenate(
        [
            shift_attn_grad[:, 0, :],
            scale_attn_grad[:, 0, :],
            gate_attn_grad,
            shift_mlp_grad[:, 0, :],
            scale_mlp_grad[:, 0, :],
            gate_mlp_grad,
        ],
        axis=-1,
    )
    mod_local = mod_grad
    mod_grad = sum(around([mod_grad] * seq_size)).astype(low)
    mod_grad = jnp.transpose(mod_grad.reshape(local_latents, dp_size, mod_share), (1, 0, 2))
    mod_grad = lax.all_to_all(mod_grad, "dp", 0, 0, tiled=True).reshape(all_latents, mod_share)
    for part in attention_sum:
        part.second(mod_local)
    for part in attention_sum:
        part.third(mod_grad)
    modulation_sum = tn(cond_rows, mod_grad)
    cond_part = nt(mod_grad, modulation_low).reshape(dp_size, local_latents * row_share)
    squares = jnp.broadcast_to(local_square, (dp_size, 128))
    back = sum_small(jnp.concatenate([cond_part, squares], axis=1))[None]
    back = after(back, *attention_sum[0].held, *attention_sum[1].held)
    back = jnp.stack(in_order(around([back] * seq_size)), axis=0)
    square_total = jnp.sum(back[:, 0, local_latents * row_share])
    masked_loss = square_total / (count_total * width)
    cond_grad = back[:, 0, : local_latents * row_share].reshape(seq_size, local_latents, row_share)
    cond_grad = jnp.transpose(cond_grad, (1, 0, 2)).reshape(local_latents, width)
    silu_pull = jax.vjp(silu_of, condition.astype(jnp.float32))[1]
    condition_grad = silu_pull(cond_grad)[0]

    mlp_sum = sum_high(after(mlp_sum, mod_grad))
    if cut_c == seq_size * proj_share:
        contraction_sum = by_distance(mlp_sum[:cut_c].reshape(seq_size, proj_share, width), 0)
    else:
        contraction_sum = narrow(mlp_sum[:cut_c], proj_share).reshape(proj_share, seq_size, -1)
        contraction_sum = by_distance(contraction_sum, 1)
    expansion_sum = mlp_sum[cut_c:]
    expansion_sum = around(
        by_distance(expansion_sum.reshape(hidden_piece, seq_size, row_share), 1)
    )
    expansion_sum = jnp.concatenate(in_order(expansion_sum), axis=0)
    contraction_sum = jnp.stack(in_order(around(contraction_sum)), axis=0)
    waits = [back], [expansion_sum, contraction_sum]
    attention_sum = jnp.concatenate([part.finish(*waits) for part in attention_sum], axis=0)
    expansion_sum = expansion_sum.T
    contraction_sum = contraction_sum.reshape(
        seq_size, proj_share, dp_size // seq_size, hidden_piece
    )
    contraction_sum = jnp.transpose(contraction_sum, (2, 0, 3, 1)).reshape(
        contraction_weight.shape
    )
    gradients = (
        modulation_sum,
        attention_sum[:qkv_share, :row_share].astype(jnp.float32).T,
        attention_sum[qkv_share:, :row_share].astype(jnp.float32).T,
        expansion_sum.astype(jnp.float32),
        contraction_sum.astype(jnp.float32),
    )

    step_rate = 0.06 / math.sqrt(all_latents * SEQ_LEN)
    masters = (
        modulation_weight,
        attention_weight,
        projection_weight,
        expansion_weight,
        contraction_weight,
    )
    moments = (
        modulation_moment,
        attention_moment,
        projection_moment,
        expansion_moment,
        contraction_moment,
    )
    averages = (
        modulation_average,
        attention_average,
        projection_average,
        expansion_average,
        contraction_average,
    )
    weight_next = []
    moment_next = []
    average_next = []
    for master, gradient, moment, average in zip(masters, gradients, moments, averages):
        moment_new = 0.5 * moment + gradient
        master_new = master - step_rate * (gradient + 0.5 * moment_new)
        weight_next.append(master_new)
        moment_next.append(moment_new)
        average_next.append(0.5 * average + 0.5 * master_new)
    return (
        block_output,
        masked_loss,
        latent_grad,
        condition_grad,
        *weight_next,
        *moment_next,
        *average_next,
    )


def solution(mesh):
    tokens_spec = P("dp", "seq", None)
    weight_spec = P("seq", "dp")
    in_specs = (
        tokens_spec,
        P("dp", None),
        tokens_spec,
        tokens_spec,
        P("dp", "seq"),
    ) + (weight_spec,) * 15
    out_specs = (tokens_spec, P(), tokens_spec, P("dp", None)) + (weight_spec,) * 15
    return jax.shard_map(body, mesh=mesh, in_specs=in_specs, out_specs=out_specs, check_vma=False)
```
